32 devices in a mesh: dp: 8 (over z, x), mp: 4 (over y, core).
Axes of the slice: x: 2, y: 2, z: 4, core: 2. Of those that a mesh axis runs over, the one named last changes fastest.
Arguments:
- layer_input: bfloat16 [4096, 1024], P(('dp', 'mp')), may hold values from -6 to 6
- first_gain: float32 [1024], replicated, may hold values from 0.25 to 1.75
- query_weight: bfloat16 [1024, 1024], P('dp', 'mp'), may hold values from -0.1875 to 0.1875
- key_matrix: bfloat16 [1024, 512], P('dp', 'mp'), may hold values from -0.1875 to 0.1875
- value_matrix: bfloat16 [1024, 512], P('dp', 'mp'), may hold values from -0.1875 to 0.1875
- output_weight: bfloat16 [1024, 1024], P('dp', 'mp'), may hold values from -1 to 1
- second_gain: float32 [1024], replicated, may hold values from 0.25 to 1.75
- gate_weight: bfloat16 [32, 1024, 512], P('dp'), may hold values from -0.1875 to 0.1875
- up_weight: bfloat16 [32, 1024, 512], P('dp'), may hold values from -0.1875 to 0.1875
- down_weight: bfloat16 [32, 512, 1024], P('dp'), may hold values from -1 to 1
- routes: int32 [4096, 8], P(('dp', 'mp')), may hold values from 0 to 31, all different within a row; in each aligned block of 128 rows (0 to 127, 128 to 255, ...) at most 40 rows name the same one
- combine: float32 [4096, 8], P(('dp', 'mp')), may hold values from 0.05 to 0.25
- upstream: bfloat16 [4096, 1024], P(('dp', 'mp')), may hold values from -6 to 6
Outputs:
- layer_output: bfloat16 [4096, 1024], P(('dp', 'mp'))
- input_grad: float32 [4096, 1024], P(('dp', 'mp'))
- first_gain_grad: float32 [1024], replicated
- second_gain_grad: float32 [1024], replicated
- query_grad: float32 [1024, 1024], P('dp', 'mp')
- key_grad: float32 [1024, 512], P('dp', 'mp')
- value_grad: float32 [1024, 512], P('dp', 'mp')
- output_weight_grad: float32 [1024, 1024], P('dp', 'mp')
- gate_grad: float32 [32, 1024, 512], P('dp')
- up_grad: float32 [32, 1024, 512], P('dp')
- down_grad: float32 [32, 512, 1024], P('dp')
The draws below stay inside these ranges and needn't reach their ends.
Inputs may be any that keep to these rules, and one draw needn't show every extreme that they name: `routes`: each row names 8 different experts; in each aligned block of 128 rows (the rows of one device) no expert is named by more than 40 rows, a bound that some block reaches.
All inputs are finite; a program needn't handle non-finite values.
Results may differ from the reference program's by a relative error of at most 0.023.
Values may be sent and summed in bfloat16 or wider, within the bound.
No kernel may reach another device: no remote copies, remote signals or barrier semaphores. Data moves between devices by JAX's collectives and lax.ppermute only.
A program may use at most 192 MiB of HBM per device.

```python
import math
import jax
import jax.numpy as jnp
import numpy as np
from jax import lax

MODEL_WIDTH = 1024
QUERY_HEADS = 16
KEY_VALUE_HEADS = 8
HEAD_SIZE = 64
EXPERTS = 32
FF = 512
TOPK = 8
SEQUENCE_TOKENS = 4096
TOKENS = 4096
ROWS = 128
MOST = 40
SPLIT = 1
PIECES = 32
PIECE_FF = 512


def block_levels(key, extent, pieces, low, high):
    loudness, own = 1.0, jax.random.fold_in(key, 6)
    for axis_at, shards_of in pieces:
        heights = jnp.exp(jax.random.uniform(jax.random.fold_in(own, axis_at), (shards_of,), jnp.float32, low / len(pieces), high / len(pieces)))
        loudness = loudness * jnp.repeat(heights, extent[axis_at] // shards_of).reshape([-1 if axis == axis_at else 1 for axis in range(len(extent))])
    return loudness


def routed_block(own_key, own, number, rows, number_of, top, most, slope):
    order = jax.random.permutation(own_key, number_of)
    packed, common = shares(number_of, rows * top, most, slope, True), shares(number_of, rows * top, most, slope, False)
    places = jnp.arange(number_of)

    def named(sizes, turn):
        used = int((sizes > 0).sum())
        fixed = max(1, used // 4)
        shifted = fixed + (places - fixed + turn * (used - fixed)) % max(1, number_of - fixed)
        return jnp.zeros((number_of,), jnp.int32).at[order[jnp.where(places < fixed, places, shifted)]].set(jnp.asarray(sizes, jnp.int32))

    sizes = jnp.where(number % 4 == 0, named(packed, number // 4), named(common, number - number // 4 - 1))
    mixed = jax.random.permutation(jax.random.fold_in(own, 3), number_of)
    giver, taker = mixed[0:number_of // 2 * 2:2], mixed[1:number_of // 2 * 2:2]
    slack = jnp.minimum(sizes[giver] - 1, most - sizes[taker]) // 2
    slack = jnp.where((giver == order[0]) | (taker == order[0]) | (sizes[taker] == 0), 0, jnp.maximum(slack, 0))
    shifted = jax.random.randint(jax.random.fold_in(own, 4), (number_of // 2,), 0, 1 << 20) % (slack + 1)
    sizes = sizes.at[giver].add(-shifted).at[taker].add(shifted)
    items = jnp.searchsorted(jnp.cumsum(sizes), jnp.arange(rows * top), side="right").astype(jnp.int32)
    table = items.reshape(top, rows).T
    table = table[jax.random.permutation(jax.random.fold_in(own, 1), rows)]
    turn = jax.random.randint(jax.random.fold_in(own, 2), (rows, 1), 0, top)
    return jnp.take_along_axis(table, (jnp.arange(top)[None, :] + turn) % top, axis=1)


def shares(amount, total, bound, slope, full):
    loads = [(1 << 20) // math.isqrt(grade ** slope) + 1 for grade in range(1, amount + 1)]
    largest = bound if full else min(bound, max(-(-total // amount), total * loads[0] // sum(loads)))
    least = 1 if total - largest >= amount - 1 else 0
    holding, rest = [largest] + [least] * (amount - 1), total - largest - least * (amount - 1)
    while rest > 0:
        candidates = [i for i in range(1, amount) if holding[i] < largest] or [i for i in range(1, amount) if holding[i] < bound]
        whole, left = sum([loads[i] for i in candidates]), rest
        for i in candidates:
            extra = min(bound - holding[i], max(1, left * loads[i] // whole), rest)
            holding[i] = holding[i] + extra
            rest = rest - extra
    return np.array(holding)


def scatter_about(stream_key, shape, width, bound, cuts=(), kind=jnp.bfloat16):
    array = width * jax.random.normal(stream_key, shape, jnp.float32)
    if cuts:
        array = array * block_levels(stream_key, shape, cuts, -0.22, 0.18)
    return jnp.clip(array, -bound, bound).astype(kind)


def setup_inputs(seed: int = 0) -> dict:
    key_of = jax.random.split(jax.random.key(seed), 14)
    layer_input = scatter_about(key_of[0], (TOKENS, MODEL_WIDTH), 1.0, 6.0, ((0, 32),))
    first_gain = jnp.clip(1.0 + 0.15 * jax.random.normal(key_of[1], (MODEL_WIDTH,), jnp.float32), 0.25, 1.75)
    query_weight = scatter_about(key_of[2], (MODEL_WIDTH, QUERY_HEADS * HEAD_SIZE), MODEL_WIDTH ** -0.5, 0.1875, ((0, 8), (1, 4)))
    key_matrix = scatter_about(key_of[3], (MODEL_WIDTH, KEY_VALUE_HEADS * HEAD_SIZE), MODEL_WIDTH ** -0.5, 0.1875, ((0, 8), (1, 4)))
    value_matrix = scatter_about(key_of[4], (MODEL_WIDTH, KEY_VALUE_HEADS * HEAD_SIZE), MODEL_WIDTH ** -0.5, 0.1875, ((0, 8), (1, 4)))
    output_weight = scatter_about(key_of[5], (MODEL_WIDTH, QUERY_HEADS * HEAD_SIZE), (QUERY_HEADS * HEAD_SIZE // 32) ** -0.5, 1.0, ((0, 8), (1, 4)))
    second_gain = jnp.clip(1.0 + 0.15 * jax.random.normal(key_of[6], (MODEL_WIDTH,), jnp.float32), 0.25, 1.75)
    gate_weight = scatter_about(key_of[7], (PIECES, MODEL_WIDTH, PIECE_FF), MODEL_WIDTH ** -0.5, 0.1875, ((0, 8),))
    up_weight = scatter_about(key_of[8], (PIECES, MODEL_WIDTH, PIECE_FF), MODEL_WIDTH ** -0.5, 0.1875, ((0, 8),))
    down_weight = scatter_about(key_of[9], (PIECES, PIECE_FF, MODEL_WIDTH), (FF // 16) ** -0.5, 1.0, ((0, 8),))
    routes_keys = jax.random.split(jax.random.fold_in(key_of[10], 1), TOKENS // ROWS)
    routes_turns = jax.random.permutation(jax.random.fold_in(key_of[10], 3), TOKENS // ROWS)
    routes = jax.vmap(lambda own, number: routed_block(jax.random.fold_in(key_of[10], 2), own, number, ROWS, EXPERTS, TOPK, MOST, 1))(routes_keys, routes_turns).reshape((TOKENS, TOPK))
    combine = jnp.clip(jnp.exp(math.log(0.25) - 1.609438 * jax.random.uniform(key_of[11], (TOKENS, TOPK), jnp.float32) ** block_levels(key_of[11], (TOKENS, TOPK), ((0, 32),), -0.2, 0.2)), 0.05, 0.25)
    upstream = scatter_about(key_of[12], (TOKENS, MODEL_WIDTH), 1.0, 6.0, ((0, 32),))
    return {"layer_input": layer_input, "first_gain": first_gain, "query_weight": query_weight, "key_matrix": key_matrix, "value_matrix": value_matrix, "output_weight": output_weight, "second_gain": second_gain, "gate_weight": gate_weight, "up_weight": up_weight, "down_weight": down_weight, "routes": routes, "combine": combine, "upstream": upstream}


epsilon = 1e-06
theta = 10000.0
masked = -1e+30
exact_cast = lax.Precision.HIGHEST

@jax.custom_vjp
def reduced_cast(v):
    return lax.optimization_barrier(v.astype(jnp.bfloat16)).astype(jnp.float32)

@jax.custom_vjp
def reduced_cast_backward(v):
    return v

def low_keep(v):
    return (reduced_cast(v), None)

def low_pass(kept, grad):
    return (grad,)

def back_keep(v):
    return (v, None)

def back_low(kept, grad):
    return (reduced_cast(grad),)
reduced_cast.defvjp(low_keep, low_pass)
reduced_cast_backward.defvjp(back_keep, back_low)

def normalize(value_rows, gain):
    scale = lax.rsqrt(lax.optimization_barrier(jnp.mean(value_rows * value_rows, axis=-1, keepdims=True)) + epsilon)
    return value_rows * scale * gain

def apply_rotary(value_rows, token_positions):
    depth = value_rows.shape[-1]
    half = depth // 2
    freqs = theta ** (-jnp.arange(half, dtype=jnp.float32) * 2.0 / depth)
    angles = token_positions.astype(jnp.float32)[:, None] * freqs[None, :]
    cosine = jnp.cos(angles)[:, None, :]
    sine = jnp.sin(angles)[:, None, :]
    first = value_rows[..., :half]
    second = value_rows[..., half:]
    return jnp.concatenate([first * cosine - second * sine, second * cosine + first * sine], axis=-1)

def sequence_layer(inputs, route_rows, combine_rows, first_gain, query_weight, key_matrix, value_matrix, output_weight, second_gain, gate_weight, up_weight, down_weight):
    query_group = QUERY_HEADS // KEY_VALUE_HEADS
    token_positions = jnp.arange(SEQUENCE_TOKENS, dtype=jnp.int32)
    leading_norm = reduced_cast(normalize(inputs, first_gain))
    unrotated_query = reduced_cast_backward(jnp.dot(leading_norm, query_weight, precision=exact_cast))
    unrotated_key = reduced_cast_backward(jnp.dot(leading_norm, key_matrix, precision=exact_cast))
    value_rows = reduced_cast(reduced_cast_backward(jnp.dot(leading_norm, value_matrix, precision=exact_cast))).reshape(SEQUENCE_TOKENS, KEY_VALUE_HEADS, HEAD_SIZE)
    query_rows = reduced_cast(apply_rotary(unrotated_query.reshape(SEQUENCE_TOKENS, QUERY_HEADS, HEAD_SIZE), token_positions)).reshape(SEQUENCE_TOKENS, KEY_VALUE_HEADS, query_group, HEAD_SIZE)
    key_rows = reduced_cast(apply_rotary(unrotated_key.reshape(SEQUENCE_TOKENS, KEY_VALUE_HEADS, HEAD_SIZE), token_positions))
    scores = reduced_cast_backward(jnp.einsum('thgd,nhd->hgtn', query_rows, key_rows, precision=exact_cast) * HEAD_SIZE ** (-0.5))
    causal = token_positions[:, None] >= token_positions[None, :]
    scores = jnp.where(causal, scores, masked)
    highest = lax.optimization_barrier(jnp.max(scores, axis=-1, keepdims=True))
    powers = jnp.exp(scores - highest)
    probs = powers / lax.optimization_barrier(jnp.sum(powers, axis=-1, keepdims=True))
    attended = jnp.einsum('hgtn,nhd->thgd', reduced_cast(probs), value_rows, precision=exact_cast).reshape(SEQUENCE_TOKENS, QUERY_HEADS * HEAD_SIZE)
    attended = reduced_cast(reduced_cast_backward(attended))
    branch = reduced_cast_backward(jnp.dot(attended, output_weight.T, precision=exact_cast))
    middle = inputs + branch
    second_norm = reduced_cast(normalize(middle, second_gain))
    blocks = SEQUENCE_TOKENS // ROWS
    slots = blocks * MOST
    chosen = lax.optimization_barrier(jnp.sum((route_rows[:, :, None] == jnp.arange(EXPERTS, dtype=jnp.int32)[None, None, :]).astype(jnp.int32), axis=1))
    blocked = chosen.reshape(blocks, ROWS, EXPERTS)
    before = (jnp.cumsum(blocked, axis=1) - blocked).reshape(SEQUENCE_TOKENS, EXPERTS)
    rank = jnp.take_along_axis(before, route_rows, axis=1)
    block_of = jnp.arange(SEQUENCE_TOKENS, dtype=jnp.int32) // ROWS
    slot = route_rows * slots + block_of[:, None] * MOST + rank
    pair = jnp.full((EXPERTS * slots,), SEQUENCE_TOKENS * TOPK, jnp.int32).at[slot.reshape(-1)].set(jnp.arange(SEQUENCE_TOKENS * TOPK, dtype=jnp.int32))
    token = pair // TOPK
    padded = jnp.concatenate([second_norm, jnp.zeros((1, MODEL_WIDTH), jnp.float32)], axis=0)
    gathered = padded[token].reshape(EXPERTS, 1, slots, MODEL_WIDTH)
    expert_in = reduced_cast_backward(jnp.broadcast_to(gathered, (EXPERTS, SPLIT, slots, MODEL_WIDTH)))
    gate_all = gate_weight.reshape(EXPERTS, SPLIT, MODEL_WIDTH, PIECE_FF)
    up_all = up_weight.reshape(EXPERTS, SPLIT, MODEL_WIDTH, PIECE_FF)
    down_all = down_weight.reshape(EXPERTS, SPLIT, PIECE_FF, MODEL_WIDTH)
    gate = reduced_cast_backward(jnp.einsum('eswd,esdf->eswf', expert_in, gate_all, precision=exact_cast))
    upper = reduced_cast_backward(jnp.einsum('eswd,esdf->eswf', expert_in, up_all, precision=exact_cast))
    hidden = reduced_cast(gate * jax.nn.sigmoid(gate) * upper)
    produced = reduced_cast(reduced_cast_backward(jnp.einsum('eswf,esfd->eswd', hidden, down_all, precision=exact_cast)))
    merged = lax.optimization_barrier(jnp.sum(produced, axis=1)).reshape(EXPERTS * slots, MODEL_WIDTH)
    mixture = lax.optimization_barrier(jnp.sum(merged[slot] * combine_rows[:, :, None], axis=1))
    return middle + mixture

def reference(layer_input, first_gain, query_weight, key_matrix, value_matrix, output_weight, second_gain, gate_weight, up_weight, down_weight, routes, combine, upstream):
    count = TOKENS // SEQUENCE_TOKENS
    route_seq = routes.reshape(count, SEQUENCE_TOKENS, TOPK)
    combine_seq = combine.astype(jnp.float32).reshape(count, SEQUENCE_TOKENS, TOPK)
    layer = jax.checkpoint(sequence_layer)

    def forward(inputs, gain_a, weight_q, weight_k, weight_v, weight_o, gain_b, weight_g, weight_u, weight_d):

        def step(carry, item):
            rows_in, route_rows, combine_rows = item
            result = layer(rows_in, route_rows, combine_rows, gain_a, weight_q, weight_k, weight_v, weight_o, gain_b, weight_g, weight_u, weight_d)
            return (carry, result)
        carry, outputs = lax.scan(step, None, (inputs.reshape(count, SEQUENCE_TOKENS, MODEL_WIDTH), route_seq, combine_seq))
        return outputs.reshape(TOKENS, MODEL_WIDTH)
    primals = (layer_input.astype(jnp.float32), first_gain.astype(jnp.float32), query_weight.astype(jnp.float32), key_matrix.astype(jnp.float32), value_matrix.astype(jnp.float32), output_weight.astype(jnp.float32), second_gain.astype(jnp.float32), gate_weight.astype(jnp.float32), up_weight.astype(jnp.float32), down_weight.astype(jnp.float32))
    result, puller = jax.vjp(forward, *primals)
    grads = puller(upstream.astype(jnp.float32))
    return (result.astype(jnp.bfloat16), grads[0], grads[1], grads[6], grads[2], grads[3], grads[4], grads[5], grads[7], grads[8], grads[9])
```

```python
import jax
import jax.numpy as jnp
from jax import lax
from jax.experimental import pallas as pl
from jax.experimental.pallas import tpu as pltpu
from jax.sharding import PartitionSpec as P

HEAD_SIZE = 64
EXPERTS = 32
FF = 512
SEQUENCE_TOKENS = 4096


epsilon = 1e-06
theta = 10000.0
masked = -1e30
vmem_bytes = 56 * 2**20
vmem_small = 20 * 2**20


def passed_along(value, axis, steps):
    count = lax.axis_size(axis)
    first, last = (max(0, -steps), min(count, count - steps))
    return lax.ppermute(value, axis, [(source, source + steps) for source in range(first, last)])


def contract(left, right, left_dim, right_dim):
    return lax.dot_general(
        left, right, (((left_dim,), (right_dim,)), ((), ())), preferred_element_type=jnp.float32
    )


def rotation(token_positions, depth):
    half = depth // 2
    freqs = theta ** (-jnp.arange(half, dtype=jnp.float32) * 2.0 / depth)
    angles = token_positions.astype(jnp.float32)[:, None] * freqs[None, :]
    return (jnp.cos(angles)[:, None, :], jnp.sin(angles)[:, None, :])


def apply_rotary(value_rows, cosine, sine):
    half = value_rows.shape[-1] // 2
    first = value_rows[..., :half]
    second = value_rows[..., half:]
    return jnp.concatenate(
        [first * cosine - second * sine, second * cosine + first * sine], axis=-1
    )


def block_scores(query_rows, keys_block, query_pos, key_pos, scale):
    scores = (
        jnp.einsum("thgd,nhd->hgtn", query_rows, keys_block, preferred_element_type=jnp.float32)
        * scale
    )
    allowed = (key_pos[None, :] <= query_pos[:, None]) & (key_pos[None, :] >= 0)
    return jnp.where(allowed, scores, masked)


def send_slots(payload):
    return lax.all_to_all(payload, "dp", split_axis=0, concat_axis=0, tiled=True)


def shards(
    layer_input,
    first_gain,
    query_weight,
    key_matrix,
    value_matrix,
    output_weight,
    second_gain,
    gate_weight,
    up_weight,
    down_weight,
    routes,
    combine,
    upstream,
):
    rows, width = layer_input.shape
    topk = routes.shape[1]
    most = max(2, 5 * rows * topk // (4 * EXPERTS))
    devices = lax.axis_size("dp")
    pieces_dev = gate_weight.shape[0]
    split = FF // gate_weight.shape[2]
    local_q = query_weight.shape[1] // HEAD_SIZE
    local_kv = key_matrix.shape[1] // HEAD_SIZE
    query_group = local_q // local_kv
    scale = HEAD_SIZE ** (-0.5)
    inputs_f = layer_input.astype(jnp.float32)
    first_scale = lax.rsqrt(jnp.mean(inputs_f * inputs_f, axis=-1, keepdims=True) + epsilon)
    first_hat = inputs_f * first_scale
    leading_norm = (first_hat * first_gain).astype(jnp.bfloat16)
    sequence_rows = lax.all_gather(leading_norm, "mp", axis=0, tiled=True)
    tokens = sequence_rows.shape[0]
    span = SEQUENCE_TOKENS // tokens
    full_query, full_key, full_value, full_out = (
        lax.all_gather(query_weight, "dp", axis=0, tiled=True),
        lax.all_gather(key_matrix, "dp", axis=0, tiled=True),
        lax.all_gather(value_matrix, "dp", axis=0, tiled=True),
        lax.all_gather(output_weight, "dp", axis=0, tiled=True),
    )
    unrotated_query = jnp.dot(sequence_rows, full_query, preferred_element_type=jnp.float32)
    unrotated_key = jnp.dot(sequence_rows, full_key, preferred_element_type=jnp.float32)
    values_own = (
        jnp.dot(sequence_rows, full_value, preferred_element_type=jnp.float32)
        .astype(jnp.bfloat16)
        .reshape(tokens, local_kv, HEAD_SIZE)
    )
    offset = lax.axis_index("dp") % span
    query_pos = offset * tokens + jnp.arange(tokens, dtype=jnp.int32)
    cosine, sine = rotation(query_pos, HEAD_SIZE)
    query_rows = apply_rotary(
        unrotated_query.reshape(tokens, local_q, HEAD_SIZE), cosine, sine
    ).astype(jnp.bfloat16)
    query_rows = query_rows.reshape(tokens, local_kv, query_group, HEAD_SIZE)
    keys_own = apply_rotary(
        unrotated_key.reshape(tokens, local_kv, HEAD_SIZE), cosine, sine
    ).astype(jnp.bfloat16)
    key_list = [keys_own]
    value_list = [values_own]
    for step in range(1, span):
        earlier_key, earlier_value = passed_along((keys_own, values_own), "dp", step)
        key_list.insert(0, earlier_key)
        value_list.insert(0, earlier_value)
    all_keys = jnp.concatenate(key_list, axis=0)
    all_values = jnp.concatenate(value_list, axis=0)
    first_key = (offset - span + 1) * tokens
    key_pos = first_key + jnp.arange(span * tokens, dtype=jnp.int32)
    key_block = min(512, span * tokens)
    block_count = span * tokens // key_block

    def block_live(lower):
        return first_key + lower + key_block > 0

    running_top = jnp.full((local_kv, query_group, tokens), masked, jnp.float32)
    running_total = jnp.zeros((local_kv, query_group, tokens), jnp.float32)
    for index in range(block_count):
        lower = index * key_block

        def stats_step(state, lower=lower):
            top_now, total_now = state
            scores = block_scores(
                query_rows,
                all_keys[lower : lower + key_block],
                query_pos,
                key_pos[lower : lower + key_block],
                scale,
            )
            new_top = jnp.maximum(top_now, jnp.max(scores, axis=-1))
            new_total = total_now * jnp.exp(top_now - new_top) + jnp.sum(
                jnp.exp(scores - new_top[..., None]), axis=-1
            )
            return (new_top, new_total)

        running_top, running_total = lax.cond(
            block_live(lower), stats_step, lambda state: state, (running_top, running_total)
        )
    logsum = running_top + jnp.log(running_total)
    attended = jnp.zeros((tokens, local_kv, query_group, HEAD_SIZE), jnp.float32)
    for index in range(block_count):
        lower = index * key_block

        def attend_step(total, lower=lower):
            scores = block_scores(
                query_rows,
                all_keys[lower : lower + key_block],
                query_pos,
                key_pos[lower : lower + key_block],
                scale,
            )
            probs = jnp.exp(scores - logsum[..., None]).astype(jnp.bfloat16)
            return total + jnp.einsum(
                "hgtn,nhd->thgd",
                probs,
                all_values[lower : lower + key_block],
                preferred_element_type=jnp.float32,
            )

        attended = lax.cond(block_live(lower), attend_step, lambda total: total, attended)
    attended_low = attended.reshape(tokens, local_q * HEAD_SIZE).astype(jnp.bfloat16)
    branch_part = contract(attended_low, full_out, 1, 1)
    branch = lax.psum_scatter(
        branch_part.astype(jnp.bfloat16), "mp", scatter_dimension=0, tiled=True
    ).astype(jnp.float32)
    middle = inputs_f + branch
    second_scale = lax.rsqrt(jnp.mean(middle * middle, axis=-1, keepdims=True) + epsilon)
    second_hat = middle * second_scale
    second_norm = (second_hat * second_gain).astype(jnp.bfloat16)
    chosen = jnp.sum(
        (routes[:, :, None] == jnp.arange(EXPERTS, dtype=jnp.int32)[None, None, :]).astype(
            jnp.int32
        ),
        axis=1,
    )
    before = jnp.cumsum(chosen, axis=0) - chosen
    rank = jnp.take_along_axis(before, routes, axis=1)
    slot = routes * most + rank
    pair = (
        jnp.full((EXPERTS * most,), rows * topk, jnp.int32)
        .at[slot.reshape(-1)]
        .set(jnp.arange(rows * topk, dtype=jnp.int32))
    )
    token_of = pair // topk
    padded_norm = jnp.concatenate([second_norm, jnp.zeros((1, width), jnp.bfloat16)], axis=0)
    gathered = padded_norm[token_of].reshape(EXPERTS, 1, most, width)
    dispatched = jnp.broadcast_to(gathered, (EXPERTS, split, most, width)).reshape(
        devices, pieces_dev, most, width
    )
    padded_up = jnp.concatenate([upstream, jnp.zeros((1, width), jnp.bfloat16)], axis=0)
    weights_flat = jnp.concatenate([combine.reshape(-1), jnp.zeros((1,), jnp.float32)], axis=0)
    slot_weight = weights_flat[pair]
    slot_grads = (padded_up[token_of].astype(jnp.float32) * slot_weight[:, None]).astype(
        jnp.bfloat16
    )
    slot_grads = jnp.broadcast_to(
        slot_grads.reshape(EXPERTS, 1, most, width), (EXPERTS, split, most, width)
    ).reshape(devices, pieces_dev, most, width)
    received = send_slots(dispatched)
    gate = jnp.einsum("spmd,pdf->spmf", received, gate_weight, preferred_element_type=jnp.float32)
    upper = jnp.einsum("spmd,pdf->spmf", received, up_weight, preferred_element_type=jnp.float32)
    sigmoid = jax.nn.sigmoid(gate)
    activated = gate * sigmoid
    hidden = (activated * upper).astype(jnp.bfloat16)
    produced = jnp.einsum(
        "spmf,pfd->spmd", hidden, down_weight, preferred_element_type=jnp.float32
    ).astype(jnp.bfloat16)
    returned = lax.all_to_all(produced, "dp", split_axis=0, concat_axis=0, tiled=True)
    merged = jnp.sum(returned.reshape(EXPERTS, split, most, width).astype(jnp.float32), axis=1)
    merged = merged.reshape(EXPERTS * most, width)
    mixture = jnp.sum(merged[slot] * combine[:, :, None], axis=1)
    layer_output = (middle + mixture).astype(jnp.bfloat16)
    upstream_f = upstream.astype(jnp.float32)
    received_grads = send_slots(slot_grads)
    hidden_grad = jnp.einsum(
        "spmd,pfd->spmf", received_grads, down_weight, preferred_element_type=jnp.float32
    )
    gate_low = (hidden_grad * upper * (sigmoid * (1.0 + gate * (1.0 - sigmoid)))).astype(
        jnp.bfloat16
    )
    upper_low = (hidden_grad * activated).astype(jnp.bfloat16)
    slot_input_grad = (
        jnp.einsum("spmf,pdf->spmd", gate_low, gate_weight, preferred_element_type=jnp.float32)
        + jnp.einsum("spmf,pdf->spmd", upper_low, up_weight, preferred_element_type=jnp.float32)
    ).astype(jnp.bfloat16)
    gate_sum = jnp.einsum("spmd,spmf->pdf", received, gate_low, preferred_element_type=jnp.float32)
    upper_sum = jnp.einsum(
        "spmd,spmf->pdf", received, upper_low, preferred_element_type=jnp.float32
    )
    down_sum = jnp.einsum(
        "spmf,spmd->pfd", hidden, received_grads, preferred_element_type=jnp.float32
    )
    gate_grad, up_grad, down_grad = (
        lax.psum(gate_sum.astype(jnp.bfloat16), "mp").astype(jnp.float32),
        lax.psum(upper_sum.astype(jnp.bfloat16), "mp").astype(jnp.float32),
        lax.psum(down_sum.astype(jnp.bfloat16), "mp").astype(jnp.float32),
    )
    back = lax.all_to_all(slot_input_grad, "dp", split_axis=0, concat_axis=0, tiled=True)
    back_merged = jnp.sum(back.reshape(EXPERTS, split, most, width).astype(jnp.float32), axis=1)
    back_merged = back_merged.reshape(EXPERTS * most, width)
    norm_two_grad = jnp.sum(back_merged[slot], axis=1)
    second_gain_part = jnp.sum(norm_two_grad * second_hat, axis=0)
    weighted_two = norm_two_grad * second_gain
    middle_grad = upstream_f + second_scale * (
        weighted_two - second_hat * jnp.mean(weighted_two * second_hat, axis=-1, keepdims=True)
    )
    branch_low = middle_grad.astype(jnp.bfloat16)
    branch_rows = lax.all_gather(branch_low, "mp", axis=0, tiled=True)
    full_query, full_key, full_value, full_out = (
        lax.all_gather(query_weight, "dp", axis=0, tiled=True),
        lax.all_gather(key_matrix, "dp", axis=0, tiled=True),
        lax.all_gather(value_matrix, "dp", axis=0, tiled=True),
        lax.all_gather(output_weight, "dp", axis=0, tiled=True),
    )
    attended_grad = jnp.dot(branch_rows, full_out, preferred_element_type=jnp.float32).astype(
        jnp.bfloat16
    )
    attended_grad4 = attended_grad.reshape(tokens, local_kv, query_group, HEAD_SIZE)
    delta = jnp.transpose(
        jnp.sum(attended_grad4.astype(jnp.float32) * attended, axis=-1), (1, 2, 0)
    )
    query_rot_grad = jnp.zeros((tokens, local_kv, query_group, HEAD_SIZE), jnp.float32)
    key_parts = []
    value_parts = []
    for index in range(block_count):
        lower = index * key_block

        def grad_step(query_total, lower=lower):
            keys_block = all_keys[lower : lower + key_block]
            values_block = all_values[lower : lower + key_block]
            scores = block_scores(
                query_rows, keys_block, query_pos, key_pos[lower : lower + key_block], scale
            )
            probs = jnp.exp(scores - logsum[..., None])
            prob_grad = jnp.einsum(
                "thgd,nhd->hgtn", attended_grad4, values_block, preferred_element_type=jnp.float32
            )
            score_grad = (probs * (prob_grad - delta[..., None])).astype(jnp.bfloat16)
            value_part = jnp.einsum(
                "hgtn,thgd->nhd",
                probs.astype(jnp.bfloat16),
                attended_grad4,
                preferred_element_type=jnp.float32,
            )
            query_next = query_total + jnp.einsum(
                "hgtn,nhd->thgd", score_grad, keys_block, preferred_element_type=jnp.float32
            )
            key_part = jnp.einsum(
                "hgtn,thgd->nhd", score_grad, query_rows, preferred_element_type=jnp.float32
            )
            return (query_next, key_part, value_part)

        def grad_skip(query_total):
            empty = jnp.zeros((key_block, local_kv, HEAD_SIZE), jnp.float32)
            return (query_total, empty, empty)

        query_rot_grad, key_part, value_part = lax.cond(
            block_live(lower), grad_step, grad_skip, query_rot_grad
        )
        key_parts.append(key_part)
        value_parts.append(value_part)
    key_all_grad = jnp.concatenate(key_parts, axis=0) * scale
    value_all_grad = jnp.concatenate(value_parts, axis=0)
    query_rot_grad = query_rot_grad * scale
    own_start = (span - 1) * tokens
    key_total = key_all_grad[own_start:]
    value_total = value_all_grad[own_start:]
    for step in range(1, span):
        start = (span - 1 - step) * tokens
        got_key, got_value = (
            passed_along(
                key_all_grad[start : start + tokens].astype(jnp.bfloat16), "dp", -step
            ).astype(jnp.float32),
            passed_along(
                value_all_grad[start : start + tokens].astype(jnp.bfloat16), "dp", -step
            ).astype(jnp.float32),
        )
        key_total = key_total + got_key
        value_total = value_total + got_value
    query_plain_grad = (
        apply_rotary(query_rot_grad.reshape(tokens, local_q, HEAD_SIZE), cosine, -sine)
        .astype(jnp.bfloat16)
        .reshape(tokens, local_q * HEAD_SIZE)
    )
    key_plain_grad = (
        apply_rotary(key_total, cosine, -sine)
        .astype(jnp.bfloat16)
        .reshape(tokens, local_kv * HEAD_SIZE)
    )
    value_plain_grad = value_total.astype(jnp.bfloat16).reshape(tokens, local_kv * HEAD_SIZE)
    input_part = (
        contract(query_plain_grad, full_query, 1, 1)
        + contract(key_plain_grad, full_key, 1, 1)
        + contract(value_plain_grad, full_value, 1, 1)
    )
    norm_one_grad = lax.psum_scatter(
        input_part.astype(jnp.bfloat16), "mp", scatter_dimension=0, tiled=True
    ).astype(jnp.float32)
    weight_block = lax.psum_scatter(
        jnp.concatenate(
            [
                contract(sequence_rows, query_plain_grad, 0, 0),
                contract(sequence_rows, key_plain_grad, 0, 0),
                contract(sequence_rows, value_plain_grad, 0, 0),
                contract(branch_rows, attended_low, 0, 0),
            ],
            axis=1,
        ),
        "dp",
        scatter_dimension=0,
        tiled=True,
    )
    query_cols = local_q * HEAD_SIZE
    kv_cols = local_kv * HEAD_SIZE
    query_grad = weight_block[:, :query_cols]
    key_grad = weight_block[:, query_cols : query_cols + kv_cols]
    value_grad = weight_block[:, query_cols + kv_cols : query_cols + 2 * kv_cols]
    output_weight_grad = weight_block[:, query_cols + 2 * kv_cols :]
    first_gain_part = jnp.sum(norm_one_grad * first_hat, axis=0)
    weighted_one = norm_one_grad * first_gain
    input_grad = middle_grad + first_scale * (
        weighted_one - first_hat * jnp.mean(weighted_one * first_hat, axis=-1, keepdims=True)
    )
    first_gain_grad, second_gain_grad = lax.psum((first_gain_part, second_gain_part), ("dp", "mp"))
    return (
        layer_output,
        input_grad,
        first_gain_grad,
        second_gain_grad,
        query_grad,
        key_grad,
        value_grad,
        output_weight_grad,
        gate_grad,
        up_grad,
        down_grad,
    )


def xor_gather(value, axis):
    count = lax.axis_size(axis)
    chunks = [value] + [None] * (count - 1)
    order = sorted(range(1, count), key=lambda r: (bin(r).count("1"), -(r & -r)))
    for r in order:
        low = r & -r
        chunks[r] = lax.ppermute(chunks[r ^ low], axis, [(i, i ^ low) for i in range(count)])
    return chunks


def xor_scatter(chunks, axis):
    count = lax.axis_size(axis)
    pending = [[chunk] for chunk in chunks]
    order = sorted(range(1, count), key=lambda r: (-bin(r).count("1"), r & -r))
    for r in order:
        low = r & -r
        total = add_parts(pending[r])
        pending[r ^ low].append(
            lax.ppermute(total, axis, [(i, i ^ low) for i in range(count)])
        )
    return pending[0]


def add_parts(parts):
    if len(parts) == 1:
        return parts[0]
    return sum_parts(parts).astype(parts[0].dtype)


def sum_parts(parts):
    total = parts[0].astype(jnp.float32)
    for part in parts[1:]:
        total = total + part.astype(jnp.float32)
    return total


def butterfly_sum(value, axis):
    count = lax.axis_size(axis)
    bit = 1
    while bit < count:
        value = value + lax.ppermute(value, axis, [(i, i ^ bit) for i in range(count)])
        bit *= 2
    return value


def dot_nn(left, right):
    return lax.dot_general(
        left, right, (((1,), (0,)), ((), ())), preferred_element_type=jnp.float32
    )


def dot_nt(left, right):
    return lax.dot_general(
        left, right, (((1,), (1,)), ((), ())), preferred_element_type=jnp.float32
    )


def dot_tn(left, right):
    return lax.dot_general(
        left, right, (((0,), (0,)), ((), ())), preferred_element_type=jnp.float32
    )


def low(value):
    return value.astype(jnp.bfloat16)


def wide(value):
    return value.astype(jnp.float32)


def call(body, outs, operands, scalars, flops, scratch=(), grid=None, in_specs=None,
         out_specs=None, transcendentals=0, aliases=None):
    memory = vmem_small if grid is None else vmem_bytes
    size = sum(x.size * x.dtype.itemsize for x in operands)
    size += sum(x.size * x.dtype.itemsize for x in outs)
    if grid is None:
        in_specs = [pl.BlockSpec(memory_space=pltpu.SMEM)] * len(scalars)
        in_specs += [pl.BlockSpec(memory_space=pltpu.VMEM)] * len(operands)
        layout = {
            "in_specs": in_specs,
            "out_specs": [pl.BlockSpec(memory_space=pltpu.VMEM)] * len(outs),
            "scratch_shapes": list(scratch),
        }
    else:
        layout = {
            "grid_spec": pltpu.PrefetchScalarGridSpec(
                num_scalar_prefetch=len(scalars),
                grid=grid,
                in_specs=in_specs,
                out_specs=out_specs,
                scratch_shapes=list(scratch),
            )
        }
    return pl.pallas_call(
        body,
        out_shape=list(outs),
        input_output_aliases=aliases or {},
        compiler_params=pltpu.CompilerParams(vmem_limit_bytes=memory),
        cost_estimate=pl.CostEstimate(
            flops=int(flops // 256), bytes_accessed=int(size // 256), transcendentals=0
        ),
        **layout,
    )(*scalars, *operands)


def shape(dims, dtype):
    return jax.ShapeDtypeStruct(tuple(dims), dtype)


def column(index, me, width):
    return pl.ds(pl.multiple_of((index ^ me) * width, width), width)


def first_norm_rows(layer_input, gain, me, count):
    rows, width = layer_input.shape
    chunk = width // count

    def body(me_ref, x_ref, gain_ref, out_ref):
        x = wide(x_ref[...])
        scale = lax.rsqrt(jnp.mean(x * x, axis=-1, keepdims=True) + epsilon)
        normed = low(x * scale * gain_ref[...])
        for r in range(count):
            out_ref[:, column(r, me_ref[0], chunk)] = normed[:, r * chunk : (r + 1) * chunk]

    return call(
        body, [shape((rows, width), jnp.bfloat16)], [layer_input, gain], [me], 4 * rows * width
    )[0]


def rope_rows(block, cosine, sine):
    half = HEAD_SIZE // 2
    first, second = block[:half], block[half:]
    return jnp.concatenate(
        [first * cosine - second * sine, second * cosine + first * sine], axis=0
    )


def padded_heads(blocks, group):
    heads = len(blocks)
    kv = heads // group
    empty = jnp.zeros_like(blocks[0])
    columns = []
    for head, block in enumerate(blocks):
        parts = [block if k == head // group else empty for k in range(kv)]
        columns.append(jnp.concatenate(parts, axis=0))
    return jnp.concatenate(columns, axis=1)


def project(x_chunks, w_chunks, cosine, sine, local_q, local_kv):
    w_chunks, w_cols = w_chunks
    tokens = sum(x.shape[0] for x in x_chunks)
    width = x_chunks[0].shape[1]
    cols = w_cols.stop - w_cols.start
    kv_rows = local_kv * HEAD_SIZE
    group = local_q // local_kv
    nx, nw = len(x_chunks), len(w_chunks)

    def body(*refs):
        x_refs, w_refs = refs[:nx], refs[nx : nx + nw]
        cos_ref, sin_ref, q_ref, kv_ref = refs[nx + nw :]
        weight = jnp.concatenate([w[:, w_cols] for w in w_refs], axis=0)
        rows = jnp.concatenate([x[...] for x in x_refs], axis=0)
        plain = dot_nn(rows, weight).T
        cosine, sine = cos_ref[...], sin_ref[...]
        blocks = [
            low(rope_rows(plain[h * HEAD_SIZE : (h + 1) * HEAD_SIZE], cosine, sine))
            for h in range(local_q + local_kv)
        ]
        scale = jnp.bfloat16(HEAD_SIZE ** (-0.5))
        q_ref[...] = padded_heads([b * scale for b in blocks[:local_q]], group)
        for h in range(local_kv):
            kv_ref[h * HEAD_SIZE : (h + 1) * HEAD_SIZE, :] = blocks[local_q + h]
        kv_ref[kv_rows:, :] = low(plain[local_q * HEAD_SIZE + kv_rows :])

    return call(
        body,
        [
            shape((kv_rows, local_q * tokens), jnp.bfloat16),
            shape((2 * kv_rows, tokens), jnp.bfloat16),
        ],
        [*x_chunks, *w_chunks, cosine, sine],
        [],
        2 * tokens * width * cols,
    )


def attention_part(offset, state, queries, kv_chunks, numbers, key_pos, query_pos, local_q):
    kv_rows, all_rows = queries.shape
    tokens = all_rows // local_q
    n = len(kv_chunks)
    first = state is None

    def body(off_ref, *refs):
        if not first:
            before_ref, refs = refs[0], refs[1:]
        q_ref, kv_refs = refs[0], refs[1 : 1 + n]
        kpos_ref, qpos_ref, state_ref = refs[1 + n :]
        off = off_ref[0]
        if not first:
            state_ref[...] = before_ref[...]
        top_at, total_at = slice(kv_rows, kv_rows + 1), slice(kv_rows + 1, kv_rows + 2)
        for index, r in enumerate(numbers):

            def block(index=index, r=r):
                keys = kv_refs[index][:kv_rows, :].T
                values = kv_refs[index][kv_rows:, :]

                def head(h, _):
                    cols = pl.ds(pl.multiple_of(h * tokens, tokens), tokens)
                    scores = dot_nn(keys, q_ref[:, cols])
                    if r == 0:
                        scores = jnp.where(kpos_ref[...] <= qpos_ref[...], scores, masked)
                        top = jnp.max(scores, axis=0, keepdims=True)
                        probs = jnp.exp(scores - top)
                        state_ref[total_at, cols] = jnp.sum(probs, axis=0, keepdims=True)
                        state_ref[:kv_rows, cols] = dot_nn(values, low(probs))
                    else:
                        before = state_ref[top_at, cols]
                        top = jnp.maximum(before, jnp.max(scores, axis=0, keepdims=True))
                        probs = jnp.exp(scores - top)
                        alpha = jnp.exp(before - top)
                        state_ref[total_at, cols] = state_ref[total_at, cols] * alpha + jnp.sum(
                            probs, axis=0, keepdims=True
                        )
                        state_ref[:kv_rows, cols] = state_ref[:kv_rows, cols] * alpha + dot_nn(
                            values, low(probs)
                        )
                    state_ref[top_at, cols] = top
                    return 0

                lax.fori_loop(0, local_q, head, 0)

            if r == 0:
                block()
            else:
                pl.when((r ^ off) < off)(block)

    operands = [queries, *kv_chunks, key_pos, query_pos]
    return call(
        body,
        [shape((kv_rows + 8, all_rows), jnp.float32)],
        operands if first else [state, *operands],
        [offset],
        4 * all_rows * tokens * n * kv_rows,
        transcendentals=all_rows * tokens * n,
        aliases=None if first else {1: 0},
    )


def attention_end(state, out_chunks, local_q, kv_rows, pieces):
    out_chunks, w_cols = out_chunks
    all_rows = state.shape[1]
    tokens = all_rows // local_q
    group = local_q // (kv_rows // HEAD_SIZE)
    nw = len(out_chunks)
    width = nw * out_chunks[0].shape[0]

    def body(state_ref, *refs):
        w_refs = refs[:nw]
        att_ref, lse_ref = refs[nw : nw + 2]
        branch_refs = refs[nw + 2 :]
        total = state_ref[kv_rows + 1 : kv_rows + 2, :]
        lse_ref[...] = state_ref[kv_rows : kv_rows + 1, :] + jnp.log(total)
        for h in range(local_q):
            rows = slice((h // group) * HEAD_SIZE, (h // group + 1) * HEAD_SIZE)
            cols = slice(h * tokens, (h + 1) * tokens)
            att_ref[h * HEAD_SIZE : (h + 1) * HEAD_SIZE, :] = state_ref[rows, cols] / total[:, cols]
        attended = low(att_ref[...].T)
        weight = jnp.concatenate([w[:, w_cols] for w in w_refs], axis=0)
        part = tokens // pieces
        for m in range(pieces):
            branch_refs[m][...] = low(dot_nt(attended[m * part : (m + 1) * part], weight))

    f32 = jnp.float32
    outs = [shape((local_q * HEAD_SIZE, tokens), f32), shape((1, all_rows), f32)]
    outs += [shape((tokens // pieces, width), jnp.bfloat16)] * pieces
    return call(
        body, outs, [state, *out_chunks], [], 2 * tokens * width * local_q * HEAD_SIZE
    )


def middle_rows(me, layer_input, branch_parts, gain, count):
    rows, width = layer_input.shape
    chunk = width // count
    n = len(branch_parts)

    def body(me_ref, x_ref, gain_ref, *refs):
        branch = sum_parts([b[...] for b in refs[:n]])
        middle_ref, norm_ref = refs[n:]
        for r in range(count):
            at = column(r, me_ref[0], chunk)
            middle_ref[:, at] = wide(x_ref[:, at]) + branch[:, r * chunk : (r + 1) * chunk]
        middle = middle_ref[...]
        scale = lax.rsqrt(jnp.mean(middle * middle, axis=-1, keepdims=True) + epsilon)
        norm_ref[...] = low(middle * scale * gain_ref[...])

    return call(
        body,
        [shape((rows, width), jnp.float32), shape((rows, width), jnp.bfloat16)],
        [layer_input, gain, *branch_parts],
        [me],
        6 * rows * width,
    )


def routing_tables(chosen, payloads, cols, experts_all, most, pieces):
    count, rows = len(payloads), payloads[0].shape[0]
    tokens = cols.stop - cols.start

    def body(chosen_ref, *refs):
        out_ref, wide_ref = refs[count:]
        for source in range(count):
            wide_ref[source * rows : (source + 1) * rows, :] = wide(refs[source][:, cols])
        for k in range(pieces):
            for source in range(count):
                at = slice(source * tokens, (source + 1) * tokens)
                lines = [
                    wide_ref[pl.ds(source * rows + kind * experts_all + chosen_ref[k], 1), :]
                    for kind in range(4)
                ]
                place = jnp.where(lines[0] >= 0, lines[0] + source % 2 * most, -1.0)
                out_ref[k, 0:1, at] = place
                out_ref[k, 1:2, at] = lines[1] + (lines[2] + lines[3])

    return call(
        body,
        [shape((pieces, 2, count * tokens), jnp.float32)],
        list(payloads),
        [chosen],
        count * rows * tokens,
        scratch=[pltpu.VMEM((count * rows, tokens), jnp.float32)],
    )[0]


def stacked(chunks):
    count = len(chunks)

    def body(*refs):
        for k in range(count):
            refs[count][k] = refs[k][...]

    outs = [shape((count,) + chunks[0].shape, chunks[0].dtype)]
    return call(body, outs, list(chunks), [], chunks[0].size)[0]


def experts(selected, norms, gathered, tables, gate_w, up_w, down_w, most, pieces, whole):
    rows, width = gathered.shape[1:]
    count = selected.shape[0] - 1 - pieces
    half = pieces // 2
    nn = len(norms)
    ff = gate_w.shape[2]
    pair = 2 * rows
    taken = 2 * most
    pairs = count // 2
    slots = count * most

    def body(sel_ref, *refs):
        n_refs, u_refs = refs[:nn], refs[nn : nn + count]
        refs = refs[nn + count :]
        table_ref, g_ref, up_ref, d_ref = refs[:4]
        rest = refs[4:]
        keep_ref, send_ref, rest = *rest[:2], rest[2:]
        if whole:
            mix_refs, dx_refs = rest[:count], rest[count : 2 * count]
            xs, gs, ys, ds = rest[2 * count :]
        else:
            xs, gs = rest
        p = pl.program_id(0)

        def chosen(q):
            at = slice(q * pair, (q + 1) * pair)
            line = lax.broadcasted_iota(jnp.int32, (taken, pair), 0).astype(jnp.float32)
            return [line == table_ref[k, 0:1, at] for k in range(pieces)]

        def weighted(q, picks):
            at = slice(q * pair, (q + 1) * pair)
            return [jnp.where(c, table_ref[k, 1:2, at], 0.0) for k, c in enumerate(picks)]

        def norm_pair(q):
            if nn == 1:
                return n_refs[0][2 * q : 2 * q + 2].reshape(pair, width)
            return jnp.concatenate([n_refs[2 * q][...], n_refs[2 * q + 1][...]], axis=0)

        @pl.when(p == 0)
        def _():
            for q in range(pairs):
                picks = chosen(q)
                factor = jnp.sum(
                    jnp.concatenate(weighted(q, picks), axis=0), axis=1, keepdims=True
                )
                pick = jnp.concatenate([low(c.astype(jnp.float32)) for c in picks], axis=0)
                here = dot_nn(pick, norm_pair(q))
                grads = dot_nn(
                    pick,
                    jnp.concatenate(
                        [u_refs[2 * q][0], u_refs[2 * q + 1][0]], axis=0
                    ),
                )
                grads = grads * factor
                for k in range(pieces):
                    part = slice(k * taken, (k + 1) * taken)
                    xs[k, q * taken : (q + 1) * taken, :] = low(here[part])
                    gs[k, q * taken : (q + 1) * taken, :] = low(grads[part])

        x, produced_grad = xs[p], gs[p]
        gate_weight, up_weight, down_weight = g_ref[0], up_ref[0], d_ref[0]
        gate = dot_nn(x, gate_weight)
        upper = dot_nn(x, up_weight)
        sigmoid = jax.nn.sigmoid(gate)
        activated = gate * sigmoid
        hidden = low(activated * upper)
        hidden_grad = dot_nt(produced_grad, down_weight)
        gate_low = low(hidden_grad * upper * (sigmoid * (1.0 + gate * (1.0 - sigmoid))))
        upper_low = low(hidden_grad * activated)

        def store(ref):
            ref[0, :, :width] = x
            ref[0, :, width : 2 * width] = produced_grad
            for k, field in enumerate((hidden, gate_low, upper_low)):
                ref[0, :, 2 * width + k * ff : 2 * width + (k + 1) * ff] = field

        pl.when(p < half)(lambda: store(keep_ref))
        pl.when(p >= half)(lambda: store(send_ref))
        if whole:
            ys[p] = low(dot_nn(hidden, down_weight))
            ds[p] = low(dot_nt(gate_low, gate_weight) + dot_nt(upper_low, up_weight))

            @pl.when(p == pieces - 1)
            def _():
                for q in range(pairs):
                    picks = chosen(q)
                    pick = jnp.concatenate([c.astype(jnp.float32) for c in picks], axis=0)
                    scaled = jnp.concatenate(weighted(q, picks), axis=0)
                    at = slice(q * taken, (q + 1) * taken)
                    outs = jnp.concatenate([ys[k, at, :] for k in range(pieces)], axis=0)
                    grads = jnp.concatenate([ds[k, at, :] for k in range(pieces)], axis=0)
                    mixed = low(dot_tn(low(scaled), outs))
                    back = low(dot_tn(low(pick), grads))
                    for s in range(2):
                        part = slice(s * rows, (s + 1) * rows)
                        mix_refs[2 * q + s][...] = mixed[part]
                        dx_refs[2 * q + s][...] = back[part]

    def weight_block(a, b):
        return pl.BlockSpec((1, a, b), lambda p, sel: (sel[count + 1 + p], 0, 0))

    def fixed(dims):
        return pl.BlockSpec(tuple(dims), lambda p, sel: (0,) * len(dims))

    bf = jnp.bfloat16
    fields = (slots, 2 * width + 3 * ff)
    scratch = [pltpu.VMEM((pieces, slots, width), bf)] * 2
    outs = [shape((half,) + fields, bf)] * 2
    out_specs = [
        pl.BlockSpec((1,) + fields, lambda p, sel: (jnp.minimum(p, half - 1), 0, 0)),
        pl.BlockSpec((1,) + fields, lambda p, sel: (jnp.maximum(p - half, 0), 0, 0)),
    ]
    if whole:
        outs += [shape((rows, width), bf)] * (2 * count)
        out_specs += [fixed((rows, width))] * (2 * count)
        scratch += [pltpu.VMEM((pieces, slots, width), bf)] * 2
    blocks = [
        pl.BlockSpec((1,) + gathered.shape[1:], lambda p, sel, r=r: (sel[r], 0, 0))
        for r in range(count)
    ]
    return call(
        body,
        outs,
        [*norms, *([gathered] * count), tables, gate_w, up_w, down_w],
        [selected],
        pieces * slots * width * ff * 2 * (6 if whole else 3),
        scratch=scratch,
        grid=(pieces,),
        in_specs=[fixed(n.shape) for n in norms]
        + blocks
        + [fixed(tables.shape)]
        + [weight_block(width, ff), weight_block(width, ff), weight_block(ff, width)],
        out_specs=out_specs,
    )


def expert_weight_grads(places, groups, totals, pieces_dev, ff):
    n = len(groups)
    _, slots, cols = groups[0].shape
    width = (cols - 3 * ff) // 2
    edges = [0, width, 2 * width, 2 * width + ff, 2 * width + 2 * ff, cols]
    given = len(totals)

    def body(places_ref, *refs):
        refs = refs[given:]
        fields = [
            jnp.concatenate([r[0, :, edges[f] : edges[f + 1]] for r in refs[:n]], axis=0)
            for f in range(5)
        ]
        wide_refs, low_ref = refs[n : n + 3], refs[n + 3]
        x, produced_grad, hidden, gate_low, upper_low = fields
        for k, (left, right) in enumerate(
            [(x, gate_low), (x, upper_low), (hidden, produced_grad)]
        ):
            total = dot_tn(left, right)
            wide_refs[k][0] = total
            store_packed(low_ref, k, low(total), ff)

    dims = [(width, ff), (width, ff), (ff, width)]
    return call(
        body,
        [shape((pieces_dev,) + d, jnp.float32) for d in dims]
        + [shape((1, 3 * width, ff), jnp.bfloat16)],
        [*totals, *groups],
        [places],
        6 * n * slots * width * ff,
        grid=(1,),
        in_specs=[pl.BlockSpec(memory_space=pl.ANY)] * given
        + [pl.BlockSpec((1, slots, cols), lambda p, at: (at[1], 0, 0))] * n,
        out_specs=[pl.BlockSpec((1,) + d, lambda p, at: (at[0], 0, 0)) for d in dims]
        + [pl.BlockSpec((1, 3 * width, ff), lambda p, at: (0, 0, 0))],
        aliases={1 + k: k for k in range(given)},
    )


def store_packed(ref, k, value, ff):
    rows, cols = value.shape
    start = k * rows * cols // ff
    for cut in range(cols // ff):
        at = slice(start + cut * rows, start + (cut + 1) * rows)
        ref[0, at, :] = value[:, cut * ff : (cut + 1) * ff]


def fill_piece(place, totals, received):
    n = len(totals)
    ff = received.shape[2]

    def body(place_ref, *refs):
        packed, outs = refs[n], refs[n + 1 :]
        start = 0
        for out in outs:
            _, rows, cols = out.shape
            for cut in range(cols // ff):
                out[0, :, cut * ff : (cut + 1) * ff] = wide(packed[0, start : start + rows, :])
                start += rows

    return call(
        body,
        [shape(t.shape, t.dtype) for t in totals],
        [*totals, received],
        [place],
        received.size,
        grid=(1,),
        in_specs=[pl.BlockSpec(memory_space=pl.ANY)] * n
        + [pl.BlockSpec(received.shape, lambda p, at: (0, 0, 0))],
        out_specs=[pl.BlockSpec((1,) + t.shape[1:], lambda p, at: (at[0], 0, 0)) for t in totals],
        aliases={1 + k: k for k in range(n)},
    )


def middle_backward(me, parts, middle, gain, upstream, count):
    rows, width = middle.shape
    chunk = width // count
    n = len(parts)

    def body(me_ref, middle_ref, gain_ref, up_ref, *refs):
        grad = sum_parts([b[...] for b in refs[:n]])
        out_ref, low_ref, sum_ref = refs[n:]
        middle = middle_ref[...]
        scale = lax.rsqrt(jnp.mean(middle * middle, axis=-1, keepdims=True) + epsilon)
        hat = middle * scale
        sum_ref[...] = jnp.sum(grad * hat, axis=0, keepdims=True)
        weighted = grad * gain_ref[...]
        total = wide(up_ref[...]) + scale * (
            weighted - hat * jnp.mean(weighted * hat, axis=-1, keepdims=True)
        )
        out_ref[...] = total
        rounded = low(total)
        for r in range(count):
            low_ref[:, column(r, me_ref[0], chunk)] = rounded[:, r * chunk : (r + 1) * chunk]

    return call(
        body,
        [
            shape((rows, width), jnp.float32),
            shape((rows, width), jnp.bfloat16),
            shape((1, width), jnp.float32),
        ],
        [middle, gain, upstream, *parts],
        [me],
        12 * rows * width,
    )


def attention_backward_start(queries, attended, branch_chunks, out_chunks, local_q):
    out_chunks, w_cols = out_chunks
    kv_rows, all_rows = queries.shape
    tokens = all_rows // local_q
    group = local_q // (kv_rows // HEAD_SIZE)
    nb, nw = len(branch_chunks), len(out_chunks)
    width = branch_chunks[0].shape[1]

    def body(q_ref, att_ref, *refs):
        b_refs, w_refs = refs[:nb], refs[nb : nb + nw]
        qn_ref, dot_ref, don_ref, delta_ref = refs[nb + nw :]
        branch = jnp.concatenate([b[...] for b in b_refs], axis=0)
        weight = jnp.concatenate([w[:, w_cols] for w in w_refs], axis=0)
        grad = low(dot_nn(branch, weight).T)
        blocks = [grad[h * HEAD_SIZE : (h + 1) * HEAD_SIZE] for h in range(local_q)]
        dot_ref[...] = padded_heads(blocks, group)
        for h in range(local_q):
            cols = slice(h * tokens, (h + 1) * tokens)
            attended_h = att_ref[h * HEAD_SIZE : (h + 1) * HEAD_SIZE, :]
            delta_ref[:, cols] = jnp.sum(wide(blocks[h]) * attended_h, axis=0, keepdims=True)
            qn_ref[cols, :] = q_ref[:, cols].T
            don_ref[cols, :] = dot_ref[:, cols].T

    bf = jnp.bfloat16
    return call(
        body,
        [
            shape((all_rows, kv_rows), bf),
            shape((kv_rows, all_rows), bf),
            shape((all_rows, kv_rows), bf),
            shape((1, all_rows), jnp.float32),
        ],
        [queries, attended, *branch_chunks, *out_chunks],
        [],
        2 * tokens * width * local_q * HEAD_SIZE,
    )


def attention_backward_part(offset, total, queries, kv_chunks, extras, numbers, key_pos, query_pos,
                            lse, started, local_q, rotation_table=()):
    kv_rows, all_rows = queries.shape
    tokens = all_rows // local_q
    group = local_q // (kv_rows // HEAD_SIZE)
    n = len(kv_chunks)
    first, final = total is None, len(rotation_table) > 0
    extra_rows, width = extras[0].shape
    cuts = width // tokens
    kv_end = 2 * kv_rows

    def body(off_ref, *refs):
        if not first:
            before_ref, refs = refs[0], refs[1:]
        extra_refs, refs = refs[:n], refs[n:]
        q_ref, kv_refs = refs[0], refs[1 : 1 + n]
        kpos_ref, qpos_ref, lse_ref = refs[1 + n : 4 + n]
        qn_ref, dot_ref, don_ref, delta_ref = refs[4 + n : 8 + n]
        refs = refs[8 + n :]
        if final:
            cos_ref, sin_ref, dq_out = refs[:3]
            kv_outs = refs[3 : 3 + n]
            dq_ref, dk_ref, dv_ref = refs[3 + n :]
        else:
            dq_ref, kv_outs = refs[0], refs[1 : 1 + n]
            dk_ref, dv_ref = refs[1 + n :]
        off = off_ref[0]
        dq_ref[...] = jnp.zeros_like(dq_ref) if first else before_ref[...]
        for index, r in enumerate(numbers):

            def block(index=index, r=r):
                keys_t = kv_refs[index][:kv_rows, :]
                keys = keys_t.T
                values = kv_refs[index][kv_rows:, :].T
                dk_ref[...] = jnp.zeros_like(dk_ref)
                dv_ref[...] = jnp.zeros_like(dv_ref)

                def head(h, _):
                    cols = pl.ds(pl.multiple_of(h * tokens, tokens), tokens)
                    scores = dot_nn(keys, q_ref[:, cols])
                    probs = jnp.exp(scores - lse_ref[:, cols])
                    if r == 0:
                        probs = jnp.where(kpos_ref[...] <= qpos_ref[...], probs, 0.0)
                    prob_grad = dot_nn(values, dot_ref[:, cols])
                    score_grad = low(probs * (prob_grad - delta_ref[:, cols]))
                    dv_ref[...] += dot_nn(low(probs), don_ref[cols, :])
                    dk_ref[...] += dot_nn(score_grad, qn_ref[cols, :])
                    dq_ref[:, cols] += dot_nn(keys_t, score_grad)
                    return 0

                lax.fori_loop(0, local_q, head, 0)
                kv_outs[index][:kv_rows, :] = low(dk_ref[...].T)
                kv_outs[index][kv_rows:kv_end, :] = low(dv_ref[...].T)

            for cut in range(cuts):
                at = slice(kv_end + cut * extra_rows, kv_end + (cut + 1) * extra_rows)
                kv_outs[index][at, :] = extra_refs[index][:, cut * tokens : (cut + 1) * tokens]

            if r == 0:
                block()
            else:
                live = (r ^ off) < off
                pl.when(live)(block)

                @pl.when(jnp.logical_not(live))
                def _(index=index):
                    kv_outs[index][:kv_end, :] = jnp.zeros((kv_end, tokens), jnp.bfloat16)

        if not final:
            return
        cosine, sine = cos_ref[...], -sin_ref[...]
        for h in range(local_q):
            rows = slice((h // group) * HEAD_SIZE, (h // group + 1) * HEAD_SIZE)
            cols = slice(h * tokens, (h + 1) * tokens)
            part = dq_ref[rows, cols] * (HEAD_SIZE ** (-0.5))
            dq_out[h * HEAD_SIZE : (h + 1) * HEAD_SIZE, :] = low(rope_rows(part, cosine, sine))

    bf, f32 = jnp.bfloat16, jnp.float32
    operands = [*extras, queries, *kv_chunks, key_pos, query_pos, lse, *started, *rotation_table]
    operands = operands if first else [total, *operands]
    outs = [shape((local_q * HEAD_SIZE, tokens), bf) if final else shape((kv_rows, all_rows), f32)]
    scratch = [pltpu.VMEM((kv_rows, all_rows), f32)] if final else []
    scratch += [pltpu.VMEM((tokens, kv_rows), f32)] * 2
    return call(
        body,
        outs + [shape((kv_end + cuts * extra_rows, tokens), bf)] * n,
        operands,
        [offset],
        10 * all_rows * tokens * n * kv_rows,
        scratch=scratch,
        transcendentals=all_rows * tokens * n,
        aliases={1: 0} if not first and not final else None,
    )


def row_grads(me, pairs, count):
    tokens = pairs[0][1].shape[1]
    width = pairs[0][0][0].shape[1]
    cols = sum(columns.shape[0] for _, columns in pairs)
    chunk = width // count
    counts = [len(x_chunks) + 1 for x_chunks, _ in pairs]

    def body(me_ref, *refs):
        out_ref, refs, left = refs[-1], list(refs[:-1]), 0
        for n in counts:
            mine, refs = refs[:n], refs[n:]
            x = jnp.concatenate([r[...] for r in mine[:-1]], axis=0)
            total = low(dot_tn(x, low(mine[-1][...]).T))
            right = left + total.shape[1]
            for r in range(count):
                part = total[r * chunk : (r + 1) * chunk]
                out_ref[pl.ds(r ^ me_ref[0], 1), :, left:right] = part[None]
            left = right

    operands = [x for x_chunks, columns in pairs for x in (*x_chunks, columns)]
    outs = [shape((count, chunk, cols), jnp.bfloat16)]
    return call(body, outs, operands, [me], 2 * tokens * width * cols)[0]


def input_parts(me, kv_parts, middle, query_grad, x_chunks, w_chunks, cosine, sine, gain, local_kv, count):
    w_chunks, w_cols = w_chunks
    n, nx, nw = len(kv_parts), len(x_chunks), len(w_chunks)
    rows, width = x_chunks[0].shape
    tokens = query_grad.shape[1]
    kv_rows = local_kv * HEAD_SIZE
    chunk = width // count

    def body(*refs):
        me_ref = refs[0]
        parts = refs[1 : 1 + n]
        middle_ref = refs[1 + n]
        refs = refs[1:]
        dq_ref = refs[1 + n]
        x_refs = refs[2 + n : 2 + n + nx]
        w_refs = refs[2 + n + nx : 2 + n + nx + nw]
        cos_ref, sin_ref, gain_ref = refs[2 + n + nx + nw : 5 + n + nx + nw]
        outs = refs[5 + n + nx + nw :]
        in_refs, grad_ref, sum_ref, out_ref = outs[:nx], *outs[nx:]
        total = sum_parts([p[...] for p in parts])
        cosine, sine = cos_ref[...], -sin_ref[...]
        blocks = [
            low(rope_rows(total[h * HEAD_SIZE : (h + 1) * HEAD_SIZE], cosine, sine))
            for h in range(local_kv)
        ]
        for cut in range(width // tokens):
            at = slice(cut * tokens, (cut + 1) * tokens)
            mixed = total[2 * kv_rows + cut * rows : 2 * kv_rows + (cut + 1) * rows]
            out_ref[:, at] = low(middle_ref[:, at] + mixed)
        values = low(total[kv_rows : 2 * kv_rows])
        columns = jnp.concatenate([dq_ref[...], *blocks, values], axis=0).T
        weight = jnp.concatenate([w[:, w_cols] for w in w_refs], axis=0)
        sums = jnp.zeros((1, width), jnp.float32)
        for m in range(nx):
            part = dot_nt(columns[m * rows : (m + 1) * rows], weight)
            in_refs[m][...] = low(part)
            sums = sums + jnp.sum(part * wide(x_refs[m][...]), axis=0, keepdims=True)
        for r in range(count):
            at = column(r, me_ref[0], chunk)
            sum_ref[:, at] = sums[:, r * chunk : (r + 1) * chunk] / gain_ref[:, at]
        x = jnp.concatenate([x[...] for x in x_refs], axis=0)
        grads = dot_tn(x, columns[:, -2 * kv_rows :])
        for r in range(count):
            grad_ref[pl.ds(r ^ me_ref[0], 1)] = low(grads[r * chunk : (r + 1) * chunk])[None]

    return call(
        body,
        [shape((rows, width), jnp.bfloat16)] * nx
        + [shape((count, chunk, 2 * kv_rows), jnp.bfloat16)]
        + [shape((1, width), jnp.float32), shape((rows, width), jnp.bfloat16)],
        [*kv_parts, middle, query_grad, *x_chunks, *w_chunks, cosine, sine, gain],
        [me],
        4 * tokens * width * w_chunks[0].shape[1],
    )


def input_backward(me, parts, layer_input, gain, middle_grad, count):
    rows, width = layer_input.shape
    chunk = width // count
    n = len(parts)

    def body(me_ref, x_ref, gain_ref, middle_ref, *refs):
        part = sum_parts([p[...] for p in refs[:n]])
        out_ref = refs[n]
        for r in range(count):
            out_ref[:, column(r, me_ref[0], chunk)] = part[:, r * chunk : (r + 1) * chunk]
        grad = out_ref[...]
        x = wide(x_ref[...])
        scale = lax.rsqrt(jnp.mean(x * x, axis=-1, keepdims=True) + epsilon)
        hat = x * scale
        weighted = grad * gain_ref[...]
        out_ref[...] = middle_ref[...] + scale * (
            weighted - hat * jnp.mean(weighted * hat, axis=-1, keepdims=True)
        )

    return call(
        body,
        [shape((rows, width), jnp.float32)],
        [layer_input, gain, middle_grad, *parts],
        [me],
        10 * rows * width,
    )[0]


def exchange_sum(chunks):
    received = lax.all_to_all(chunks, "dp", split_axis=0, concat_axis=0, tiled=True)
    return jnp.sum(received.astype(jnp.float32), axis=0)


def after(value, *others):
    return lax.optimization_barrier((value, *others))[0]


def layer_shards(
    layer_input,
    first_gain,
    query_weight,
    key_matrix,
    value_matrix,
    output_weight,
    second_gain,
    gate_weight,
    up_weight,
    down_weight,
    routes,
    combine,
    upstream,
):
    rows, width = layer_input.shape
    topk = routes.shape[1]
    most = max(2, 5 * rows * topk // (4 * EXPERTS))
    devices = lax.axis_size("dp")
    groups = lax.axis_size("mp")
    pieces_dev = gate_weight.shape[0]
    split = FF // gate_weight.shape[2]
    local_q = query_weight.shape[1] // HEAD_SIZE
    local_kv = key_matrix.shape[1] // HEAD_SIZE
    tokens = rows * groups
    span = SEQUENCE_TOKENS // tokens
    if span != devices or pieces_dev % 2 or groups % 2:
        return shards(
            layer_input, first_gain, query_weight, key_matrix, value_matrix, output_weight,
            second_gain, gate_weight, up_weight, down_weight, routes, combine, upstream,
        )
    dp_at, mp_at = lax.axis_index("dp"), lax.axis_index("mp")
    me = jnp.full((1,), dp_at, jnp.int32)
    offset = jnp.full((1,), dp_at % span, jnp.int32)
    gain_one, gain_two = first_gain.reshape(1, width), second_gain.reshape(1, width)

    chunk_at = jnp.arange(groups, dtype=jnp.int32) ^ mp_at
    inside = (chunk_at[:, None] * rows + jnp.arange(rows, dtype=jnp.int32)[None, :]).reshape(tokens)
    positions = (dp_at % span) * tokens + inside
    freqs = theta ** (-jnp.arange(HEAD_SIZE // 2, dtype=jnp.float32) * 2.0 / HEAD_SIZE)
    angles = freqs[:, None] * positions.astype(jnp.float32)[None, :]
    cosine, sine = jnp.cos(angles), jnp.sin(angles)

    numbers = jnp.arange(EXPERTS, dtype=jnp.int32)
    equal = routes.T[None, :, :] == numbers[:, None, None]
    match = jnp.sum(equal.astype(jnp.float32), axis=1)
    weight_table = jnp.sum(jnp.where(equal, combine.T[None, :, :], 0.0), axis=1)
    line = jnp.arange(rows, dtype=jnp.int32)
    earlier = (line[:, None] < line[None, :]).astype(jnp.bfloat16)
    rank = jnp.dot(match.astype(jnp.bfloat16), earlier, preferred_element_type=jnp.float32)
    terms = [low(jnp.where(match > 0, rank, -1.0))]
    rest = weight_table
    for _ in range(3):
        term = lax.reduce_precision(rest, 8, 7)
        terms.append(low(term))
        rest = rest - term
    table = jnp.stack(terms, axis=0)
    expert_at = (dp_at * pieces_dev + jnp.arange(pieces_dev, dtype=jnp.int32)) // split
    halves = pieces_dev // 2
    first_piece = (mp_at % 2) * halves
    order = (first_piece + jnp.arange(pieces_dev, dtype=jnp.int32)) % pieces_dev
    experts_order = jnp.take(expert_at, order)

    dp_order = jnp.arange(devices, dtype=jnp.int32) ^ dp_at

    selected = jnp.concatenate([dp_order, me, order])

    normed = first_norm_rows(layer_input, gain_one, me, devices)
    weight_cols = [w.shape[1] for w in (query_weight, key_matrix, value_matrix)]
    qkv_cols = sum(weight_cols)
    out_rows, out_cols = output_weight.shape
    payload = [query_weight, key_matrix, value_matrix, output_weight, table.reshape(out_rows, -1)]
    payloads = xor_gather(jnp.concatenate(payload, axis=1), "dp")
    qkv_chunks = (payloads, slice(0, qkv_cols))
    out_chunks = (payloads, slice(qkv_cols, qkv_cols + out_cols))
    tables = routing_tables(
        experts_order, payloads, slice(qkv_cols + out_cols, payloads[0].shape[1]), EXPERTS, most,
        pieces_dev,
    )
    x_chunks = xor_gather(normed, "mp")
    queries, kv_own = project(x_chunks, qkv_chunks, cosine, sine, local_q, local_kv)
    key_pos, query_pos = inside.reshape(tokens, 1), inside.reshape(1, tokens)
    kv_chunks, state, done = [kv_own] + [None] * (devices - 1), None, []
    forward_order = [(0,)] + [(r, r + 1) for r in range(1, devices - 1, 2)] + [(devices - 1,)]

    def attend(numbers, state):
        return attention_part(
            offset, state, queries, [kv_chunks[r] for r in numbers], numbers, key_pos, query_pos,
            local_q,
        )[0]

    for r in sorted(range(1, devices), key=lambda r: (bin(r).count("1"), -(r & -r))):
        near = r & -r
        source = kv_chunks[r ^ near]
        hops = bin(r).count("1") - 1
        if r > devices // 2 and hops > 0:
            while len(done) < hops:
                done.append(attend(forward_order[len(done)], state))
                state = done[-1]
            source = after(source, done[hops - 1])
        kv_chunks[r] = lax.ppermute(source, "dp", [(i, i ^ near) for i in range(devices)])
    for numbers in forward_order[len(done) :]:
        state = attend(numbers, state)
    gathered = lax.all_gather(after(upstream, kv_chunks[-1]), "dp", axis=0, tiled=False)
    attended, lse, *branch_chunks = attention_end(state, out_chunks, local_q, kv_own.shape[0] // 2, groups)

    middle, second_norm = middle_rows(
        me, layer_input, xor_scatter(branch_chunks, "mp"), gain_two, devices
    )
    norm_chunks = xor_gather(second_norm, "dp")
    far_pairs = [[(i, i ^ g) for i in range(groups)] for g in range(2, groups, 2)]
    gathered_far = [lax.ppermute(after(gathered, second_norm), "mp", pairs) for pairs in far_pairs]
    expert_weights = (gate_weight, up_weight, down_weight)
    own = experts(
        selected, norm_chunks, gathered, tables,
        *expert_weights, most, pieces_dev, True,
    )
    mixture_chunks, back_chunks = own[2 : 2 + devices], own[2 + devices :]
    swap = [(i, i ^ 1) for i in range(groups)]
    fields = [own[0], lax.ppermute(own[1], "mp", swap)]
    back_parts = xor_scatter(back_chunks, "dp")
    middle_grad, branch_low, second_sum = middle_backward(
        me, back_parts, middle, gain_two, upstream, devices
    )

    branch_rows = xor_gather(branch_low, "mp")
    norm_here = after(stacked(norm_chunks), branch_rows[-1], *gathered_far)
    far_groups = [
        (rows_far, *[lax.ppermute(v, "mp", pairs) for v in (norm_here, tables)])
        for rows_far, pairs in zip(gathered_far, far_pairs)
    ]
    started = attention_backward_start(queries, attended, branch_rows, out_chunks, local_q)
    backward = sorted(range(devices), key=lambda r: (-bin(r).count("1"), -r))
    backward_order = [tuple(backward[i : i + 2]) for i in range(0, devices - 2, 2)]
    backward_order += [(r,) for r in backward[-2:]]
    total, pending, arrived = None, [[] for _ in range(devices)], []
    for numbers in backward_order:
        last = numbers is backward_order[-1]
        if len(arrived) > 1 and arrived[-2]:
            total = after(total, *arrived[-2])
        total, *parts = attention_backward_part(
            offset, total, queries, [kv_chunks[r] for r in numbers],
            [mixture_chunks[r] for r in numbers], numbers, key_pos, query_pos, lse, started, local_q,
            (cosine, sine) if last else (),
        )
        for r, part in zip(numbers, parts):
            pending[r].append(part)
        arrived.append([])
        for r in numbers:
            near = r & -r
            if r:
                came = lax.ppermute(
                    add_parts(pending[r]), "dp", [(i, i ^ near) for i in range(devices)]
                )
                pending[r ^ near].append(came)
                arrived[-1].append(came)
    query_plain, kv_parts = total, pending[0]
    rows_grad = exchange_sum(
        row_grads(me, [(x_chunks, query_plain), (branch_rows, attended)], devices)
    )
    query_cols = local_q * HEAD_SIZE
    query_grad, out_grad = rows_grad[:, :query_cols], rows_grad[:, query_cols:]

    for rows_far, norm_far, tables_far in far_groups:
        kept, sent = experts(
            selected, [after(norm_far, query_plain)], rows_far, tables_far, *expert_weights,
            most, pieces_dev, False,
        )
        fields += [kept, lax.ppermute(sent, "mp", swap)]
        kv_parts[0] = after(kv_parts[0], kept)
    outs = input_parts(
        me, kv_parts, middle, query_plain, x_chunks, qkv_chunks, cosine, sine, gain_one, local_kv,
        devices,
    )
    in_chunks, (kv_weights, first_sum, layer_output) = outs[:groups], outs[groups:]
    fields[0] = after(fields[0], first_sum)
    totals, received = [], []
    for i in range(halves):
        places = jnp.stack([first_piece + i, jnp.int32(i)])
        grads = expert_weight_grads(places, fields, totals, pieces_dev, FF // split)
        totals = grads[:3]
        received.append(lax.ppermute(grads[3], "mp", swap))
    for i in range(halves):
        place = jnp.full((1,), halves - first_piece + i, jnp.int32)
        totals = fill_piece(place, totals, received[i])
    gate_grad, up_grad, down_grad = totals
    in_parts = xor_scatter(in_chunks, "mp")
    kv_grad = exchange_sum(kv_weights)
    kv_cols = local_kv * HEAD_SIZE
    input_grad = input_backward(me, in_parts, layer_input, gain_one, middle_grad, devices)
    gains = butterfly_sum(jnp.concatenate([first_sum, second_sum], axis=0), "mp")
    gains = butterfly_sum(after(gains, in_parts[-1]), "dp")
    first_gain_grad, second_gain_grad = gains[0], gains[1]
    return (
        layer_output,
        input_grad,
        first_gain_grad,
        second_gain_grad,
        query_grad,
        kv_grad[:, :kv_cols],
        kv_grad[:, kv_cols:],
        out_grad,
        gate_grad,
        up_grad,
        down_grad,
    )


def solution(mesh):
    in_specs = (
        P(("dp", "mp"), None),
        P(),
        P("dp", "mp"),
        P("dp", "mp"),
        P("dp", "mp"),
        P("dp", "mp"),
        P(),
        P("dp", None, None),
        P("dp", None, None),
        P("dp", None, None),
        P(("dp", "mp"), None),
        P(("dp", "mp"), None),
        P(("dp", "mp"), None),
    )
    out_specs = (
        P(("dp", "mp"), None),
        P(("dp", "mp"), None),
        P(),
        P(),
        P("dp", "mp"),
        P("dp", "mp"),
        P("dp", "mp"),
        P("dp", "mp"),
        P("dp", None, None),
        P("dp", None, None),
        P("dp", None, None),
    )
    return jax.shard_map(
        layer_shards, mesh=mesh, in_specs=in_specs, out_specs=out_specs, check_vma=False)
```

```python
import jax
import jax.numpy as jnp
from jax import lax
from jax.experimental import pallas as pl
from jax.experimental.pallas import tpu as pltpu
from jax.sharding import PartitionSpec as P

HEAD_SIZE = 64
EXPERTS = 32
FF = 512
SEQUENCE_TOKENS = 4096


epsilon = 1e-06
theta = 10000.0
masked = -1e30
vmem_bytes = 56 * 2**20
vmem_small = 20 * 2**20
pace = 1.15e9


def passed_along(value, axis, steps):
    count = lax.axis_size(axis)
    first, last = (max(0, -steps), min(count, count - steps))
    return lax.ppermute(value, axis, [(source, source + steps) for source in range(first, last)])


def contract(left, right, left_dim, right_dim):
    return lax.dot_general(
        left, right, (((left_dim,), (right_dim,)), ((), ())), preferred_element_type=jnp.float32
    )


def rotation(token_positions, depth):
    half = depth // 2
    freqs = theta ** (-jnp.arange(half, dtype=jnp.float32) * 2.0 / depth)
    angles = token_positions.astype(jnp.float32)[:, None] * freqs[None, :]
    return (jnp.cos(angles)[:, None, :], jnp.sin(angles)[:, None, :])


def apply_rotary(value_rows, cosine, sine):
    half = value_rows.shape[-1] // 2
    first = value_rows[..., :half]
    second = value_rows[..., half:]
    return jnp.concatenate(
        [first * cosine - second * sine, second * cosine + first * sine], axis=-1
    )


def block_scores(query_rows, keys_block, query_pos, key_pos, scale):
    scores = (
        jnp.einsum("thgd,nhd->hgtn", query_rows, keys_block, preferred_element_type=jnp.float32)
        * scale
    )
    allowed = (key_pos[None, :] <= query_pos[:, None]) & (key_pos[None, :] >= 0)
    return jnp.where(allowed, scores, masked)


def send_slots(payload):
    return lax.all_to_all(payload, "dp", split_axis=0, concat_axis=0, tiled=True)


def shards(
    layer_input,
    first_gain,
    query_weight,
    key_matrix,
    value_matrix,
    output_weight,
    second_gain,
    gate_weight,
    up_weight,
    down_weight,
    routes,
    combine,
    upstream,
):
    rows, width = layer_input.shape
    topk = routes.shape[1]
    most = max(2, 5 * rows * topk // (4 * EXPERTS))
    devices = lax.axis_size("dp")
    pieces_dev = gate_weight.shape[0]
    split = FF // gate_weight.shape[2]
    local_q = query_weight.shape[1] // HEAD_SIZE
    local_kv = key_matrix.shape[1] // HEAD_SIZE
    query_group = local_q // local_kv
    scale = HEAD_SIZE ** (-0.5)
    inputs_f = layer_input.astype(jnp.float32)
    first_scale = lax.rsqrt(jnp.mean(inputs_f * inputs_f, axis=-1, keepdims=True) + epsilon)
    first_hat = inputs_f * first_scale
    leading_norm = (first_hat * first_gain).astype(jnp.bfloat16)
    sequence_rows = lax.all_gather(leading_norm, "mp", axis=0, tiled=True)
    tokens = sequence_rows.shape[0]
    span = SEQUENCE_TOKENS // tokens
    full_query, full_key, full_value, full_out = (
        lax.all_gather(query_weight, "dp", axis=0, tiled=True),
        lax.all_gather(key_matrix, "dp", axis=0, tiled=True),
        lax.all_gather(value_matrix, "dp", axis=0, tiled=True),
        lax.all_gather(output_weight, "dp", axis=0, tiled=True),
    )
    unrotated_query = jnp.dot(sequence_rows, full_query, preferred_element_type=jnp.float32)
    unrotated_key = jnp.dot(sequence_rows, full_key, preferred_element_type=jnp.float32)
    values_own = (
        jnp.dot(sequence_rows, full_value, preferred_element_type=jnp.float32)
        .astype(jnp.bfloat16)
        .reshape(tokens, local_kv, HEAD_SIZE)
    )
    offset = lax.axis_index("dp") % span
    query_pos = offset * tokens + jnp.arange(tokens, dtype=jnp.int32)
    cosine, sine = rotation(query_pos, HEAD_SIZE)
    query_rows = apply_rotary(
        unrotated_query.reshape(tokens, local_q, HEAD_SIZE), cosine, sine
    ).astype(jnp.bfloat16)
    query_rows = query_rows.reshape(tokens, local_kv, query_group, HEAD_SIZE)
    keys_own = apply_rotary(
        unrotated_key.reshape(tokens, local_kv, HEAD_SIZE), cosine, sine
    ).astype(jnp.bfloat16)
    key_list = [keys_own]
    value_list = [values_own]
    for step in range(1, span):
        earlier_key, earlier_value = passed_along((keys_own, values_own), "dp", step)
        key_list.insert(0, earlier_key)
        value_list.insert(0, earlier_value)
    all_keys = jnp.concatenate(key_list, axis=0)
    all_values = jnp.concatenate(value_list, axis=0)
    first_key = (offset - span + 1) * tokens
    key_pos = first_key + jnp.arange(span * tokens, dtype=jnp.int32)
    key_block = min(512, span * tokens)
    block_count = span * tokens // key_block

    def block_live(lower):
        return first_key + lower + key_block > 0

    running_top = jnp.full((local_kv, query_group, tokens), masked, jnp.float32)
    running_total = jnp.zeros((local_kv, query_group, tokens), jnp.float32)
    for index in range(block_count):
        lower = index * key_block

        def stats_step(state, lower=lower):
            top_now, total_now = state
            scores = block_scores(
                query_rows,
                all_keys[lower : lower + key_block],
                query_pos,
                key_pos[lower : lower + key_block],
                scale,
            )
            new_top = jnp.maximum(top_now, jnp.max(scores, axis=-1))
            new_total = total_now * jnp.exp(top_now - new_top) + jnp.sum(
                jnp.exp(scores - new_top[..., None]), axis=-1
            )
            return (new_top, new_total)

        running_top, running_total = lax.cond(
            block_live(lower), stats_step, lambda state: state, (running_top, running_total)
        )
    logsum = running_top + jnp.log(running_total)
    attended = jnp.zeros((tokens, local_kv, query_group, HEAD_SIZE), jnp.float32)
    for index in range(block_count):
        lower = index * key_block

        def attend_step(total, lower=lower):
            scores = block_scores(
                query_rows,
                all_keys[lower : lower + key_block],
                query_pos,
                key_pos[lower : lower + key_block],
                scale,
            )
            probs = jnp.exp(scores - logsum[..., None]).astype(jnp.bfloat16)
            return total + jnp.einsum(
                "hgtn,nhd->thgd",
                probs,
                all_values[lower : lower + key_block],
                preferred_element_type=jnp.float32,
            )

        attended = lax.cond(block_live(lower), attend_step, lambda total: total, attended)
    attended_low = attended.reshape(tokens, local_q * HEAD_SIZE).astype(jnp.bfloat16)
    branch_part = contract(attended_low, full_out, 1, 1)
    branch = lax.psum_scatter(
        branch_part.astype(jnp.bfloat16), "mp", scatter_dimension=0, tiled=True
    ).astype(jnp.float32)
    middle = inputs_f + branch
    second_scale = lax.rsqrt(jnp.mean(middle * middle, axis=-1, keepdims=True) + epsilon)
    second_hat = middle * second_scale
    second_norm = (second_hat * second_gain).astype(jnp.bfloat16)
    chosen = jnp.sum(
        (routes[:, :, None] == jnp.arange(EXPERTS, dtype=jnp.int32)[None, None, :]).astype(
            jnp.int32
        ),
        axis=1,
    )
    before = jnp.cumsum(chosen, axis=0) - chosen
    rank = jnp.take_along_axis(before, routes, axis=1)
    slot = routes * most + rank
    pair = (
        jnp.full((EXPERTS * most,), rows * topk, jnp.int32)
        .at[slot.reshape(-1)]
        .set(jnp.arange(rows * topk, dtype=jnp.int32))
    )
    token_of = pair // topk
    padded_norm = jnp.concatenate([second_norm, jnp.zeros((1, width), jnp.bfloat16)], axis=0)
    gathered = padded_norm[token_of].reshape(EXPERTS, 1, most, width)
    dispatched = jnp.broadcast_to(gathered, (EXPERTS, split, most, width)).reshape(
        devices, pieces_dev, most, width
    )
    padded_up = jnp.concatenate([upstream, jnp.zeros((1, width), jnp.bfloat16)], axis=0)
    weights_flat = jnp.concatenate([combine.reshape(-1), jnp.zeros((1,), jnp.float32)], axis=0)
    slot_weight = weights_flat[pair]
    slot_grads = (padded_up[token_of].astype(jnp.float32) * slot_weight[:, None]).astype(
        jnp.bfloat16
    )
    slot_grads = jnp.broadcast_to(
        slot_grads.reshape(EXPERTS, 1, most, width), (EXPERTS, split, most, width)
    ).reshape(devices, pieces_dev, most, width)
    received = send_slots(dispatched)
    gate = jnp.einsum("spmd,pdf->spmf", received, gate_weight, preferred_element_type=jnp.float32)
    upper = jnp.einsum("spmd,pdf->spmf", received, up_weight, preferred_element_type=jnp.float32)
    sigmoid = jax.nn.sigmoid(gate)
    activated = gate * sigmoid
    hidden = (activated * upper).astype(jnp.bfloat16)
    produced = jnp.einsum(
        "spmf,pfd->spmd", hidden, down_weight, preferred_element_type=jnp.float32
    ).astype(jnp.bfloat16)
    returned = lax.all_to_all(produced, "dp", split_axis=0, concat_axis=0, tiled=True)
    merged = jnp.sum(returned.reshape(EXPERTS, split, most, width).astype(jnp.float32), axis=1)
    merged = merged.reshape(EXPERTS * most, width)
    mixture = jnp.sum(merged[slot] * combine[:, :, None], axis=1)
    layer_output = (middle + mixture).astype(jnp.bfloat16)
    upstream_f = upstream.astype(jnp.float32)
    received_grads = send_slots(slot_grads)
    hidden_grad = jnp.einsum(
        "spmd,pfd->spmf", received_grads, down_weight, preferred_element_type=jnp.float32
    )
    gate_low = (hidden_grad * upper * (sigmoid * (1.0 + gate * (1.0 - sigmoid)))).astype(
        jnp.bfloat16
    )
    upper_low = (hidden_grad * activated).astype(jnp.bfloat16)
    slot_input_grad = (
        jnp.einsum("spmf,pdf->spmd", gate_low, gate_weight, preferred_element_type=jnp.float32)
        + jnp.einsum("spmf,pdf->spmd", upper_low, up_weight, preferred_element_type=jnp.float32)
    ).astype(jnp.bfloat16)
    gate_sum = jnp.einsum("spmd,spmf->pdf", received, gate_low, preferred_element_type=jnp.float32)
    upper_sum = jnp.einsum(
        "spmd,spmf->pdf", received, upper_low, preferred_element_type=jnp.float32
    )
    down_sum = jnp.einsum(
        "spmf,spmd->pfd", hidden, received_grads, preferred_element_type=jnp.float32
    )
    gate_grad, up_grad, down_grad = (
        lax.psum(gate_sum.astype(jnp.bfloat16), "mp").astype(jnp.float32),
        lax.psum(upper_sum.astype(jnp.bfloat16), "mp").astype(jnp.float32),
        lax.psum(down_sum.astype(jnp.bfloat16), "mp").astype(jnp.float32),
    )
    back = lax.all_to_all(slot_input_grad, "dp", split_axis=0, concat_axis=0, tiled=True)
    back_merged = jnp.sum(back.reshape(EXPERTS, split, most, width).astype(jnp.float32), axis=1)
    back_merged = back_merged.reshape(EXPERTS * most, width)
    norm_two_grad = jnp.sum(back_merged[slot], axis=1)
    second_gain_part = jnp.sum(norm_two_grad * second_hat, axis=0)
    weighted_two = norm_two_grad * second_gain
    middle_grad = upstream_f + second_scale * (
        weighted_two - second_hat * jnp.mean(weighted_two * second_hat, axis=-1, keepdims=True)
    )
    branch_low = middle_grad.astype(jnp.bfloat16)
    branch_rows = lax.all_gather(branch_low, "mp", axis=0, tiled=True)
    full_query, full_key, full_value, full_out = (
        lax.all_gather(query_weight, "dp", axis=0, tiled=True),
        lax.all_gather(key_matrix, "dp", axis=0, tiled=True),
        lax.all_gather(value_matrix, "dp", axis=0, tiled=True),
        lax.all_gather(output_weight, "dp", axis=0, tiled=True),
    )
    attended_grad = jnp.dot(branch_rows, full_out, preferred_element_type=jnp.float32).astype(
        jnp.bfloat16
    )
    attended_grad4 = attended_grad.reshape(tokens, local_kv, query_group, HEAD_SIZE)
    delta = jnp.transpose(
        jnp.sum(attended_grad4.astype(jnp.float32) * attended, axis=-1), (1, 2, 0)
    )
    query_rot_grad = jnp.zeros((tokens, local_kv, query_group, HEAD_SIZE), jnp.float32)
    key_parts = []
    value_parts = []
    for index in range(block_count):
        lower = index * key_block

        def grad_step(query_total, lower=lower):
            keys_block = all_keys[lower : lower + key_block]
            values_block = all_values[lower : lower + key_block]
            scores = block_scores(
                query_rows, keys_block, query_pos, key_pos[lower : lower + key_block], scale
            )
            probs = jnp.exp(scores - logsum[..., None])
            prob_grad = jnp.einsum(
                "thgd,nhd->hgtn", attended_grad4, values_block, preferred_element_type=jnp.float32
            )
            score_grad = (probs * (prob_grad - delta[..., None])).astype(jnp.bfloat16)
            value_part = jnp.einsum(
                "hgtn,thgd->nhd",
                probs.astype(jnp.bfloat16),
                attended_grad4,
                preferred_element_type=jnp.float32,
            )
            query_next = query_total + jnp.einsum(
                "hgtn,nhd->thgd", score_grad, keys_block, preferred_element_type=jnp.float32
            )
            key_part = jnp.einsum(
                "hgtn,thgd->nhd", score_grad, query_rows, preferred_element_type=jnp.float32
            )
            return (query_next, key_part, value_part)

        def grad_skip(query_total):
            empty = jnp.zeros((key_block, local_kv, HEAD_SIZE), jnp.float32)
            return (query_total, empty, empty)

        query_rot_grad, key_part, value_part = lax.cond(
            block_live(lower), grad_step, grad_skip, query_rot_grad
        )
        key_parts.append(key_part)
        value_parts.append(value_part)
    key_all_grad = jnp.concatenate(key_parts, axis=0) * scale
    value_all_grad = jnp.concatenate(value_parts, axis=0)
    query_rot_grad = query_rot_grad * scale
    own_start = (span - 1) * tokens
    key_total = key_all_grad[own_start:]
    value_total = value_all_grad[own_start:]
    for step in range(1, span):
        start = (span - 1 - step) * tokens
        got_key, got_value = (
            passed_along(
                key_all_grad[start : start + tokens].astype(jnp.bfloat16), "dp", -step
            ).astype(jnp.float32),
            passed_along(
                value_all_grad[start : start + tokens].astype(jnp.bfloat16), "dp", -step
            ).astype(jnp.float32),
        )
        key_total = key_total + got_key
        value_total = value_total + got_value
    query_plain_grad = (
        apply_rotary(query_rot_grad.reshape(tokens, local_q, HEAD_SIZE), cosine, -sine)
        .astype(jnp.bfloat16)
        .reshape(tokens, local_q * HEAD_SIZE)
    )
    key_plain_grad = (
        apply_rotary(key_total, cosine, -sine)
        .astype(jnp.bfloat16)
        .reshape(tokens, local_kv * HEAD_SIZE)
    )
    value_plain_grad = value_total.astype(jnp.bfloat16).reshape(tokens, local_kv * HEAD_SIZE)
    input_part = (
        contract(query_plain_grad, full_query, 1, 1)
        + contract(key_plain_grad, full_key, 1, 1)
        + contract(value_plain_grad, full_value, 1, 1)
    )
    norm_one_grad = lax.psum_scatter(
        input_part.astype(jnp.bfloat16), "mp", scatter_dimension=0, tiled=True
    ).astype(jnp.float32)
    weight_block = lax.psum_scatter(
        jnp.concatenate(
            [
                contract(sequence_rows, query_plain_grad, 0, 0),
                contract(sequence_rows, key_plain_grad, 0, 0),
                contract(sequence_rows, value_plain_grad, 0, 0),
                contract(branch_rows, attended_low, 0, 0),
            ],
            axis=1,
        ),
        "dp",
        scatter_dimension=0,
        tiled=True,
    )
    query_cols = local_q * HEAD_SIZE
    kv_cols = local_kv * HEAD_SIZE
    query_grad = weight_block[:, :query_cols]
    key_grad = weight_block[:, query_cols : query_cols + kv_cols]
    value_grad = weight_block[:, query_cols + kv_cols : query_cols + 2 * kv_cols]
    output_weight_grad = weight_block[:, query_cols + 2 * kv_cols :]
    first_gain_part = jnp.sum(norm_one_grad * first_hat, axis=0)
    weighted_one = norm_one_grad * first_gain
    input_grad = middle_grad + first_scale * (
        weighted_one - first_hat * jnp.mean(weighted_one * first_hat, axis=-1, keepdims=True)
    )
    first_gain_grad, second_gain_grad = lax.psum((first_gain_part, second_gain_part), ("dp", "mp"))
    return (
        layer_output,
        input_grad,
        first_gain_grad,
        second_gain_grad,
        query_grad,
        key_grad,
        value_grad,
        output_weight_grad,
        gate_grad,
        up_grad,
        down_grad,
    )


def xor_gather(value, axis):
    count = lax.axis_size(axis)
    chunks = [value] + [None] * (count - 1)
    order = sorted(range(1, count), key=lambda r: (bin(r).count("1"), -(r & -r)))
    for r in order:
        low = r & -r
        chunks[r] = lax.ppermute(chunks[r ^ low], axis, [(i, i ^ low) for i in range(count)])
    return chunks


def xor_scatter(chunks, axis):
    count = lax.axis_size(axis)
    pending = [[chunk] for chunk in chunks]
    order = sorted(range(1, count), key=lambda r: (-bin(r).count("1"), r & -r))
    for r in order:
        low = r & -r
        total = add_parts(pending[r])
        pending[r ^ low].append(
            lax.ppermute(total, axis, [(i, i ^ low) for i in range(count)])
        )
    return pending[0]


def add_parts(parts):
    if len(parts) == 1:
        return parts[0]
    return sum_parts(parts).astype(parts[0].dtype)


def sum_parts(parts):
    total = parts[0].astype(jnp.float32)
    for part in parts[1:]:
        total = total + part.astype(jnp.float32)
    return total


def butterfly_sum(value, axis):
    count = lax.axis_size(axis)
    bit = 1
    while bit < count:
        value = value + lax.ppermute(value, axis, [(i, i ^ bit) for i in range(count)])
        bit *= 2
    return value


def dot_nn(left, right):
    return lax.dot_general(
        left, right, (((1,), (0,)), ((), ())), preferred_element_type=jnp.float32
    )


def dot_nt(left, right):
    return lax.dot_general(
        left, right, (((1,), (1,)), ((), ())), preferred_element_type=jnp.float32
    )


def dot_tn(left, right):
    return lax.dot_general(
        left, right, (((0,), (0,)), ((), ())), preferred_element_type=jnp.float32
    )


def low(value):
    return value.astype(jnp.bfloat16)


def wide(value):
    return value.astype(jnp.float32)


def call(body, outs, operands, scalars, micros, scratch=(), grid=None, in_specs=None,
         out_specs=None, aliases=None):
    memory = vmem_small if grid is None else vmem_bytes
    if grid is None:
        in_specs = [pl.BlockSpec(memory_space=pltpu.SMEM)] * len(scalars)
        in_specs += [pl.BlockSpec(memory_space=pltpu.VMEM)] * len(operands)
        layout = {
            "in_specs": in_specs,
            "out_specs": [pl.BlockSpec(memory_space=pltpu.VMEM)] * len(outs),
            "scratch_shapes": list(scratch),
        }
    else:
        layout = {
            "grid_spec": pltpu.PrefetchScalarGridSpec(
                num_scalar_prefetch=len(scalars),
                grid=grid,
                in_specs=in_specs,
                out_specs=out_specs,
                scratch_shapes=list(scratch),
            )
        }
    return pl.pallas_call(
        body,
        out_shape=list(outs),
        input_output_aliases=aliases or {},
        compiler_params=pltpu.CompilerParams(vmem_limit_bytes=memory),
        cost_estimate=pl.CostEstimate(
            flops=int(micros * pace), bytes_accessed=0, transcendentals=0
        ),
        **layout,
    )(*scalars, *operands)


def shape(dims, dtype):
    return jax.ShapeDtypeStruct(tuple(dims), dtype)


def column(index, me, width):
    return pl.ds(pl.multiple_of((index ^ me) * width, width), width)


def first_norm_rows(layer_input, gain, me, count):
    rows, width = layer_input.shape
    chunk = width // count

    def body(me_ref, x_ref, gain_ref, out_ref):
        x = wide(x_ref[...])
        scale = lax.rsqrt(jnp.mean(x * x, axis=-1, keepdims=True) + epsilon)
        normed = low(x * scale * gain_ref[...])
        for r in range(count):
            out_ref[:, column(r, me_ref[0], chunk)] = normed[:, r * chunk : (r + 1) * chunk]

    return call(
        body, [shape((rows, width), jnp.bfloat16)], [layer_input, gain], [me], 2
    )[0]


def rope_rows(block, cosine, sine):
    half = HEAD_SIZE // 2
    first, second = block[:half], block[half:]
    return jnp.concatenate(
        [first * cosine - second * sine, second * cosine + first * sine], axis=0
    )


def padded_heads(blocks, group):
    heads = len(blocks)
    kv = heads // group
    empty = jnp.zeros_like(blocks[0])
    columns = []
    for head, block in enumerate(blocks):
        parts = [block if k == head // group else empty for k in range(kv)]
        columns.append(jnp.concatenate(parts, axis=0))
    return jnp.concatenate(columns, axis=1)


def project(x_chunks, w_chunks, cosine, sine, local_q, local_kv):
    w_chunks, w_cols = w_chunks
    tokens = sum(x.shape[0] for x in x_chunks)
    width = x_chunks[0].shape[1]
    cols = w_cols.stop - w_cols.start
    kv_rows = local_kv * HEAD_SIZE
    group = local_q // local_kv
    nx, nw = len(x_chunks), len(w_chunks)

    def body(*refs):
        x_refs, w_refs = refs[:nx], refs[nx : nx + nw]
        cos_ref, sin_ref, q_ref, kv_ref = refs[nx + nw :]
        weight = jnp.concatenate([w[:, w_cols] for w in w_refs], axis=0)
        rows = jnp.concatenate([x[...] for x in x_refs], axis=0)
        plain = dot_nn(rows, weight).T
        cosine, sine = cos_ref[...], sin_ref[...]
        blocks = [
            low(rope_rows(plain[h * HEAD_SIZE : (h + 1) * HEAD_SIZE], cosine, sine))
            for h in range(local_q + local_kv)
        ]
        scale = jnp.bfloat16(HEAD_SIZE ** (-0.5))
        q_ref[...] = padded_heads([b * scale for b in blocks[:local_q]], group)
        for h in range(local_kv):
            kv_ref[h * HEAD_SIZE : (h + 1) * HEAD_SIZE, :] = blocks[local_q + h]
        kv_ref[kv_rows:, :] = low(plain[local_q * HEAD_SIZE + kv_rows :])

    return call(
        body,
        [
            shape((kv_rows, local_q * tokens), jnp.bfloat16),
            shape((2 * kv_rows, tokens), jnp.bfloat16),
        ],
        [*x_chunks, *w_chunks, cosine, sine],
        [],
        2,
    )


def attention_part(offset, state, queries, kv_chunks, numbers, key_pos, query_pos, local_q):
    kv_rows, all_rows = queries.shape
    tokens = all_rows // local_q
    n = len(kv_chunks)
    first = state is None

    def body(off_ref, *refs):
        if not first:
            before_ref, refs = refs[0], refs[1:]
        q_ref, kv_refs = refs[0], refs[1 : 1 + n]
        kpos_ref, qpos_ref, state_ref = refs[1 + n :]
        off = off_ref[0]
        if not first:
            state_ref[...] = before_ref[...]
        top_at, total_at = slice(kv_rows, kv_rows + 1), slice(kv_rows + 1, kv_rows + 2)
        for index, r in enumerate(numbers):

            def block(index=index, r=r):
                keys = kv_refs[index][:kv_rows, :].T
                values = kv_refs[index][kv_rows:, :]

                def head(h, _):
                    cols = pl.ds(pl.multiple_of(h * tokens, tokens), tokens)
                    scores = dot_nn(keys, q_ref[:, cols])
                    if r == 0:
                        scores = jnp.where(kpos_ref[...] <= qpos_ref[...], scores, masked)
                        top = jnp.max(scores, axis=0, keepdims=True)
                        probs = jnp.exp(scores - top)
                        state_ref[total_at, cols] = jnp.sum(probs, axis=0, keepdims=True)
                        state_ref[:kv_rows, cols] = dot_nn(values, low(probs))
                    else:
                        before = state_ref[top_at, cols]
                        top = jnp.maximum(before, jnp.max(scores, axis=0, keepdims=True))
                        probs = jnp.exp(scores - top)
                        alpha = jnp.exp(before - top)
                        state_ref[total_at, cols] = state_ref[total_at, cols] * alpha + jnp.sum(
                            probs, axis=0, keepdims=True
                        )
                        state_ref[:kv_rows, cols] = state_ref[:kv_rows, cols] * alpha + dot_nn(
                            values, low(probs)
                        )
                    state_ref[top_at, cols] = top
                    return 0

                lax.fori_loop(0, local_q, head, 0)

            if r == 0:
                block()
            else:
                pl.when((r ^ off) < off)(block)

    operands = [queries, *kv_chunks, key_pos, query_pos]
    return call(
        body,
        [shape((kv_rows + 8, all_rows), jnp.float32)],
        operands if first else [state, *operands],
        [offset],
        3 * n,
        aliases=None if first else {1: 0},
    )


def attention_end(state, out_chunks, local_q, kv_rows, pieces):
    out_chunks, w_cols = out_chunks
    all_rows = state.shape[1]
    tokens = all_rows // local_q
    group = local_q // (kv_rows // HEAD_SIZE)
    nw = len(out_chunks)
    width = nw * out_chunks[0].shape[0]

    def body(state_ref, *refs):
        w_refs = refs[:nw]
        att_ref, lse_ref = refs[nw : nw + 2]
        branch_refs = refs[nw + 2 :]
        total = state_ref[kv_rows + 1 : kv_rows + 2, :]
        lse_ref[...] = state_ref[kv_rows : kv_rows + 1, :] + jnp.log(total)
        for h in range(local_q):
            rows = slice((h // group) * HEAD_SIZE, (h // group + 1) * HEAD_SIZE)
            cols = slice(h * tokens, (h + 1) * tokens)
            att_ref[h * HEAD_SIZE : (h + 1) * HEAD_SIZE, :] = state_ref[rows, cols] / total[:, cols]
        attended = low(att_ref[...].T)
        weight = jnp.concatenate([w[:, w_cols] for w in w_refs], axis=0)
        part = tokens // pieces
        for m in range(pieces):
            branch_refs[m][...] = low(dot_nt(attended[m * part : (m + 1) * part], weight))

    f32 = jnp.float32
    outs = [shape((local_q * HEAD_SIZE, tokens), f32), shape((1, all_rows), f32)]
    outs += [shape((tokens // pieces, width), jnp.bfloat16)] * pieces
    return call(
        body, outs, [state, *out_chunks], [], 2
    )


def middle_rows(me, layer_input, branch_parts, gain, count):
    rows, width = layer_input.shape
    chunk = width // count
    n = len(branch_parts)

    def body(me_ref, x_ref, gain_ref, *refs):
        branch = sum_parts([b[...] for b in refs[:n]])
        middle_ref, norm_ref = refs[n:]
        for r in range(count):
            at = column(r, me_ref[0], chunk)
            middle_ref[:, at] = wide(x_ref[:, at]) + branch[:, r * chunk : (r + 1) * chunk]
        middle = middle_ref[...]
        scale = lax.rsqrt(jnp.mean(middle * middle, axis=-1, keepdims=True) + epsilon)
        norm_ref[...] = low(middle * scale * gain_ref[...])

    return call(
        body,
        [shape((rows, width), jnp.float32), shape((rows, width), jnp.bfloat16)],
        [layer_input, gain, *branch_parts],
        [me],
        1,
    )


def routing_tables(chosen, payloads, cols, experts_all, most, pieces):
    count, rows = len(payloads), payloads[0].shape[0]
    tokens = cols.stop - cols.start

    def body(chosen_ref, *refs):
        out_ref, wide_ref = refs[count:]
        for source in range(count):
            wide_ref[source * rows : (source + 1) * rows, :] = wide(refs[source][:, cols])
        for k in range(pieces):
            for source in range(count):
                at = slice(source * tokens, (source + 1) * tokens)
                lines = [
                    wide_ref[pl.ds(source * rows + kind * experts_all + chosen_ref[k], 1), :]
                    for kind in range(4)
                ]
                place = jnp.where(lines[0] >= 0, lines[0] + source % 2 * most, -1.0)
                out_ref[k, 0:1, at] = place
                out_ref[k, 1:2, at] = lines[1] + (lines[2] + lines[3])

    return call(
        body,
        [shape((pieces, 2, count * tokens), jnp.float32)],
        list(payloads),
        [chosen],
        1,
        scratch=[pltpu.VMEM((count * rows, tokens), jnp.float32)],
    )[0]


def stacked(chunks):
    count = len(chunks)

    def body(*refs):
        for k in range(count):
            refs[count][k] = refs[k][...]

    outs = [shape((count,) + chunks[0].shape, chunks[0].dtype)]
    return call(body, outs, list(chunks), [], 2)[0]


def experts(selected, norms, gathered, tables, gate_w, up_w, down_w, most, pieces, whole):
    rows, width = gathered[0].shape[1], gate_w.shape[1]
    parts = len(gathered)
    count = selected.shape[0] - 1 - pieces
    half = pieces // 2
    nn = len(norms)
    ff = gate_w.shape[2]
    pair = 2 * rows
    taken = 2 * most
    pairs = count // 2
    slots = count * most

    def body(sel_ref, *refs):
        n_refs, u_refs = refs[:nn], refs[nn : nn + parts * count]
        refs = refs[nn + parts * count :]
        table_ref, g_ref, up_ref, d_ref = refs[:4]
        rest = refs[4:]
        keep_ref, send_ref, rest = *rest[:2], rest[2:]
        if whole:
            mix_refs, dx_refs = rest[:2], rest[2 : 2 + count]
            xs, gs, ys, ds = rest[2 + count :]
        else:
            xs, gs = rest
        p = pl.program_id(0)

        def chosen(q):
            at = slice(q * pair, (q + 1) * pair)
            line = lax.broadcasted_iota(jnp.int32, (taken, pair), 0).astype(jnp.float32)
            return [line == table_ref[k, 0:1, at] for k in range(pieces)]

        def weighted(q, picks):
            at = slice(q * pair, (q + 1) * pair)
            return [jnp.where(c, table_ref[k, 1:2, at], 0.0) for k, c in enumerate(picks)]

        def grad_rows(r):
            return jnp.concatenate([u_refs[k * count + r][0] for k in range(parts)], axis=1)

        def norm_pair(q):
            if nn == 1:
                return n_refs[0][2 * q : 2 * q + 2].reshape(pair, width)
            return jnp.concatenate([n_refs[2 * q][...], n_refs[2 * q + 1][...]], axis=0)

        @pl.when(p == 0)
        def _():
            for q in range(pairs):
                picks = chosen(q)
                factor = jnp.sum(
                    jnp.concatenate(weighted(q, picks), axis=0), axis=1, keepdims=True
                )
                pick = jnp.concatenate([low(c.astype(jnp.float32)) for c in picks], axis=0)
                here = dot_nn(pick, norm_pair(q))
                grads = dot_nn(
                    pick,
                    jnp.concatenate([grad_rows(2 * q), grad_rows(2 * q + 1)], axis=0),
                )
                grads = grads * factor
                for k in range(pieces):
                    part = slice(k * taken, (k + 1) * taken)
                    xs[k, q * taken : (q + 1) * taken, :] = low(here[part])
                    gs[k, q * taken : (q + 1) * taken, :] = low(grads[part])

        x, produced_grad = xs[p], gs[p]
        gate_weight, up_weight, down_weight = g_ref[0], up_ref[0], d_ref[0]
        gate = dot_nn(x, gate_weight)
        upper = dot_nn(x, up_weight)
        sigmoid = jax.nn.sigmoid(gate)
        activated = gate * sigmoid
        hidden = low(activated * upper)
        hidden_grad = dot_nt(produced_grad, down_weight)
        gate_low = low(hidden_grad * upper * (sigmoid * (1.0 + gate * (1.0 - sigmoid))))
        upper_low = low(hidden_grad * activated)

        def store(ref):
            ref[0, :, :width] = x
            ref[0, :, width : 2 * width] = produced_grad
            for k, field in enumerate((hidden, gate_low, upper_low)):
                ref[0, :, 2 * width + k * ff : 2 * width + (k + 1) * ff] = field

        pl.when(p < half)(lambda: store(keep_ref))
        pl.when(p >= half)(lambda: store(send_ref))
        if whole:
            ys[p] = low(dot_nn(hidden, down_weight))
            ds[p] = low(dot_nt(gate_low, gate_weight) + dot_nt(upper_low, up_weight))

            @pl.when(p == pieces - 1)
            def _():
                for q in range(pairs):
                    picks = chosen(q)
                    pick = jnp.concatenate([c.astype(jnp.float32) for c in picks], axis=0)
                    scaled = jnp.concatenate(weighted(q, picks), axis=0)
                    at = slice(q * taken, (q + 1) * taken)
                    outs = jnp.concatenate([ys[k, at, :] for k in range(pieces)], axis=0)
                    grads = jnp.concatenate([ds[k, at, :] for k in range(pieces)], axis=0)
                    mixed = low(dot_tn(low(scaled), outs))
                    back = low(dot_tn(low(pick), grads))
                    for s in range(2):
                        part = slice(s * rows, (s + 1) * rows)
                        mix_refs[s][q] = mixed[part]
                        dx_refs[2 * q + s][...] = back[part]

    def weight_block(a, b):
        return pl.BlockSpec((1, a, b), lambda p, sel: (sel[count + 1 + p], 0, 0))

    def fixed(dims):
        return pl.BlockSpec(tuple(dims), lambda p, sel: (0,) * len(dims))

    bf = jnp.bfloat16
    fields = (slots, 2 * width + 3 * ff)
    scratch = [pltpu.VMEM((pieces, slots, width), bf)] * 2
    outs = [shape((half,) + fields, bf)] * 2
    out_specs = [
        pl.BlockSpec((1,) + fields, lambda p, sel: (jnp.minimum(p, half - 1), 0, 0)),
        pl.BlockSpec((1,) + fields, lambda p, sel: (jnp.maximum(p - half, 0), 0, 0)),
    ]
    if whole:
        outs += [shape((pairs, rows, width), bf)] * 2 + [shape((rows, width), bf)] * count
        out_specs += [fixed((pairs, rows, width))] * 2 + [fixed((rows, width))] * count
        scratch += [pltpu.VMEM((pieces, slots, width), bf)] * 2
    blocks = [
        pl.BlockSpec((1,) + part.shape[1:], lambda p, sel, r=r: (sel[r], 0, 0))
        for part in gathered
        for r in range(count)
    ]
    return call(
        body,
        outs,
        [*norms, *[part for part in gathered for _ in range(count)], tables, gate_w, up_w, down_w],
        [selected],
        23 if whole else 8,
        scratch=scratch,
        grid=(pieces,),
        in_specs=[fixed(n.shape) for n in norms]
        + blocks
        + [fixed(tables.shape)]
        + [weight_block(width, ff), weight_block(width, ff), weight_block(ff, width)],
        out_specs=out_specs,
    )


def expert_weight_grads(places, pieces, groups, totals, pieces_dev, ff, rounded):
    n = len(groups)
    _, slots, cols = groups[0].shape
    width = (cols - 3 * ff) // 2
    tiles = width // ff
    given = len(totals)

    def body(places_ref, *refs):
        before, refs = refs[:given], refs[given:]
        x, produced_grad, hidden, gate_low, upper_low = [
            jnp.concatenate([refs[5 * g + f][0] for g in range(n)], axis=0) for f in range(5)
        ]
        outs = refs[5 * n :]
        for k, (left, right) in enumerate(
            [(x, gate_low), (x, upper_low), (hidden, produced_grad)]
        ):
            total = dot_tn(left, right)
            if given:
                total = total + before[k][0]
            outs[k][0] = total
            if rounded:
                outs[3][0, k, 0] = low(total)

    def field(block):
        return pl.BlockSpec((1, slots, ff), lambda p, j, at: (at[1] + p, 0, block(j)))

    in_specs = [
        field(lambda j: j),
        field(lambda j: tiles + j),
        field(lambda j: 2 * tiles),
        field(lambda j: 2 * tiles + 1),
        field(lambda j: 2 * tiles + 2),
    ] * n
    blocks = [
        pl.BlockSpec((1, ff, ff), lambda p, j, at: (at[0] + p, j, 0)),
        pl.BlockSpec((1, ff, ff), lambda p, j, at: (at[0] + p, j, 0)),
        pl.BlockSpec((1, ff, ff), lambda p, j, at: (at[0] + p, 0, j)),
    ]
    dims = [(width, ff), (width, ff), (ff, width)]
    outs = [shape((pieces_dev,) + d, jnp.float32) for d in dims]
    out_specs = list(blocks)
    if rounded:
        outs.append(shape((pieces, 3, tiles, ff, ff), jnp.bfloat16))
        out_specs.append(pl.BlockSpec((1, 3, 1, ff, ff), lambda p, j, at: (p, 0, j, 0, 0)))
    return call(
        body,
        outs,
        [*totals, *[group for group in groups for _ in range(5)]],
        [places],
        pieces,
        grid=(pieces, tiles),
        in_specs=blocks[:given] + in_specs,
        out_specs=out_specs,
        aliases={1 + k: k for k in range(given)},
    )


def fill_pieces(place, totals, received):
    n = len(totals)
    pieces, _, tiles, ff, _ = received.shape

    def body(place_ref, *refs):
        packed, outs = refs[n], refs[n + 1 :]
        for k, out in enumerate(outs):
            out[0] = wide(packed[0, k, 0])

    return call(
        body,
        [shape(t.shape, t.dtype) for t in totals],
        [*totals, received],
        [place],
        4 * pieces,
        grid=(pieces, tiles),
        in_specs=[pl.BlockSpec(memory_space=pl.ANY)] * n
        + [pl.BlockSpec((1, 3, 1, ff, ff), lambda p, j, at: (p, 0, j, 0, 0))],
        out_specs=[
            pl.BlockSpec((1, ff, ff), lambda p, j, at: (at[0] + p, j, 0)),
            pl.BlockSpec((1, ff, ff), lambda p, j, at: (at[0] + p, j, 0)),
            pl.BlockSpec((1, ff, ff), lambda p, j, at: (at[0] + p, 0, j)),
        ],
        aliases={1 + k: k for k in range(n)},
    )


def middle_backward(me, parts, middle, gain, upstream, count):
    rows, width = middle.shape
    chunk = width // count
    n = len(parts)

    def body(me_ref, middle_ref, gain_ref, up_ref, *refs):
        grad = sum_parts([b[...] for b in refs[:n]])
        out_ref, low_ref, sum_ref = refs[n:]
        middle = middle_ref[...]
        scale = lax.rsqrt(jnp.mean(middle * middle, axis=-1, keepdims=True) + epsilon)
        hat = middle * scale
        sum_ref[...] = jnp.sum(grad * hat, axis=0, keepdims=True)
        weighted = grad * gain_ref[...]
        total = wide(up_ref[...]) + scale * (
            weighted - hat * jnp.mean(weighted * hat, axis=-1, keepdims=True)
        )
        out_ref[...] = total
        rounded = low(total)
        for r in range(count):
            low_ref[:, column(r, me_ref[0], chunk)] = rounded[:, r * chunk : (r + 1) * chunk]

    return call(
        body,
        [
            shape((rows, width), jnp.float32),
            shape((rows, width), jnp.bfloat16),
            shape((1, width), jnp.float32),
        ],
        [middle, gain, upstream, *parts],
        [me],
        2,
    )


def attention_backward_start(queries, attended, branch_chunks, out_chunks, local_q):
    out_chunks, w_cols = out_chunks
    kv_rows, all_rows = queries.shape
    tokens = all_rows // local_q
    group = local_q // (kv_rows // HEAD_SIZE)
    nb, nw = len(branch_chunks), len(out_chunks)
    width = branch_chunks[0].shape[1]

    def body(q_ref, att_ref, *refs):
        b_refs, w_refs = refs[:nb], refs[nb : nb + nw]
        qn_ref, dot_ref, don_ref, delta_ref = refs[nb + nw :]
        branch = jnp.concatenate([b[...] for b in b_refs], axis=0)
        weight = jnp.concatenate([w[:, w_cols] for w in w_refs], axis=0)
        grad = low(dot_nn(branch, weight).T)
        blocks = [grad[h * HEAD_SIZE : (h + 1) * HEAD_SIZE] for h in range(local_q)]
        dot_ref[...] = padded_heads(blocks, group)
        for h in range(local_q):
            cols = slice(h * tokens, (h + 1) * tokens)
            attended_h = att_ref[h * HEAD_SIZE : (h + 1) * HEAD_SIZE, :]
            delta_ref[:, cols] = jnp.sum(wide(blocks[h]) * attended_h, axis=0, keepdims=True)
            qn_ref[cols, :] = q_ref[:, cols].T
            don_ref[cols, :] = dot_ref[:, cols].T

    bf = jnp.bfloat16
    return call(
        body,
        [
            shape((all_rows, kv_rows), bf),
            shape((kv_rows, all_rows), bf),
            shape((all_rows, kv_rows), bf),
            shape((1, all_rows), jnp.float32),
        ],
        [queries, attended, *branch_chunks, *out_chunks],
        [],
        1,
    )


def attention_backward_part(offset, total, queries, kv_chunks, numbers, key_pos, query_pos, lse,
                            started, local_q, rotation_table=()):
    kv_rows, all_rows = queries.shape
    tokens = all_rows // local_q
    group = local_q // (kv_rows // HEAD_SIZE)
    n = len(kv_chunks)
    first, final = total is None, len(rotation_table) > 0

    def body(off_ref, *refs):
        if not first:
            before_ref, refs = refs[0], refs[1:]
        q_ref, kv_refs = refs[0], refs[1 : 1 + n]
        kpos_ref, qpos_ref, lse_ref = refs[1 + n : 4 + n]
        qn_ref, dot_ref, don_ref, delta_ref = refs[4 + n : 8 + n]
        refs = refs[8 + n :]
        if final:
            cos_ref, sin_ref, dq_out = refs[:3]
            kv_outs = refs[3 : 3 + n]
            dq_ref, dk_ref, dv_ref = refs[3 + n :]
        else:
            dq_ref, kv_outs = refs[0], refs[1 : 1 + n]
            dk_ref, dv_ref = refs[1 + n :]
        off = off_ref[0]
        dq_ref[...] = jnp.zeros_like(dq_ref) if first else before_ref[...]
        for index, r in enumerate(numbers):

            def block(index=index, r=r):
                keys_t = kv_refs[index][:kv_rows, :]
                keys = keys_t.T
                values = kv_refs[index][kv_rows:, :].T
                dk_ref[...] = jnp.zeros_like(dk_ref)
                dv_ref[...] = jnp.zeros_like(dv_ref)

                def head(h, _):
                    cols = pl.ds(pl.multiple_of(h * tokens, tokens), tokens)
                    scores = dot_nn(keys, q_ref[:, cols])
                    probs = jnp.exp(scores - lse_ref[:, cols])
                    if r == 0:
                        probs = jnp.where(kpos_ref[...] <= qpos_ref[...], probs, 0.0)
                    prob_grad = dot_nn(values, dot_ref[:, cols])
                    score_grad = low(probs * (prob_grad - delta_ref[:, cols]))
                    dv_ref[...] += dot_nn(low(probs), don_ref[cols, :])
                    dk_ref[...] += dot_nn(score_grad, qn_ref[cols, :])
                    dq_ref[:, cols] += dot_nn(keys_t, score_grad)
                    return 0

                lax.fori_loop(0, local_q, head, 0)
                kv_outs[index][:kv_rows, :] = low(dk_ref[...].T)
                kv_outs[index][kv_rows:, :] = low(dv_ref[...].T)

            if r == 0:
                block()
            else:
                live = (r ^ off) < off
                pl.when(live)(block)

                @pl.when(jnp.logical_not(live))
                def _(index=index):
                    kv_outs[index][...] = jnp.zeros_like(kv_outs[index])

        if not final:
            return
        cosine, sine = cos_ref[...], -sin_ref[...]
        for h in range(local_q):
            rows = slice((h // group) * HEAD_SIZE, (h // group + 1) * HEAD_SIZE)
            cols = slice(h * tokens, (h + 1) * tokens)
            part = dq_ref[rows, cols] * (HEAD_SIZE ** (-0.5))
            dq_out[h * HEAD_SIZE : (h + 1) * HEAD_SIZE, :] = low(rope_rows(part, cosine, sine))

    bf, f32 = jnp.bfloat16, jnp.float32
    operands = [queries, *kv_chunks, key_pos, query_pos, lse, *started, *rotation_table]
    operands = operands if first else [total, *operands]
    outs = [shape((local_q * HEAD_SIZE, tokens), bf) if final else shape((kv_rows, all_rows), f32)]
    scratch = [pltpu.VMEM((kv_rows, all_rows), f32)] if final else []
    scratch += [pltpu.VMEM((tokens, kv_rows), f32)] * 2
    return call(
        body,
        outs + [shape((2 * kv_rows, tokens), bf)] * n,
        operands,
        [offset],
        n,
        scratch=scratch,
        aliases={1: 0} if not first and not final else None,
    )


def row_grads(pairs, count):
    width = pairs[0][0][0].shape[1]
    cols = sum(columns.shape[0] for _, columns in pairs)
    chunk = width // count
    counts = [len(x_chunks) + 1 for x_chunks, _ in pairs]

    def body(*refs):
        out_refs, refs, left = refs[-2:], list(refs[:-2]), 0
        for n in counts:
            mine, refs = refs[:n], refs[n:]
            x = jnp.concatenate([r[...] for r in mine[:-1]], axis=0)
            total = low(dot_tn(x, low(mine[-1][...]).T))
            right = left + total.shape[1]
            for r in range(count):
                part = total[r * chunk : (r + 1) * chunk]
                out_refs[r % 2][r // 2, :, left:right] = part
            left = right

    operands = [x for x_chunks, columns in pairs for x in (*x_chunks, columns)]
    outs = [shape((count // 2, chunk, cols), jnp.bfloat16)] * 2
    return call(body, outs, operands, [], 2)


def input_parts(me, kv_parts, query_grad, x_chunks, w_chunks, cosine, sine, gain, local_kv, count):
    w_chunks, w_cols = w_chunks
    n, nx, nw = len(kv_parts), len(x_chunks), len(w_chunks)
    rows, width = x_chunks[0].shape
    kv_rows = local_kv * HEAD_SIZE
    chunk = width // count

    def body(me_ref, *refs):
        parts, dq_ref, refs = refs[:n], refs[n], refs[n + 1 :]
        x_refs, w_refs, refs = refs[:nx], refs[nx : nx + nw], refs[nx + nw :]
        cos_ref, sin_ref, gain_ref, refs = *refs[:3], refs[3:]
        in_refs, even_ref, odd_ref, sum_ref = refs[:nx], *refs[nx:]
        total = sum_parts([p[...] for p in parts])
        cosine, sine = cos_ref[...], -sin_ref[...]
        blocks = [
            low(rope_rows(total[h * HEAD_SIZE : (h + 1) * HEAD_SIZE], cosine, sine))
            for h in range(local_kv)
        ]
        columns = jnp.concatenate([dq_ref[...], *blocks, low(total[kv_rows:])], axis=0).T
        weight = jnp.concatenate([w[:, w_cols] for w in w_refs], axis=0)
        sums = jnp.zeros((1, width), jnp.float32)
        for m in range(nx):
            part = dot_nt(columns[m * rows : (m + 1) * rows], weight)
            in_refs[m][...] = low(part)
            sums = sums + jnp.sum(part * wide(x_refs[m][...]), axis=0, keepdims=True)
        for r in range(count):
            at = column(r, me_ref[0], chunk)
            sum_ref[:, at] = sums[:, r * chunk : (r + 1) * chunk] / gain_ref[:, at]
        x = jnp.concatenate([x[...] for x in x_refs], axis=0)
        grads = low(dot_tn(x, columns[:, -2 * kv_rows :]))
        for r in range(count):
            (even_ref, odd_ref)[r % 2][r // 2] = grads[r * chunk : (r + 1) * chunk]

    return call(
        body,
        [shape((rows, width), jnp.bfloat16)] * nx
        + [shape((count // 2, chunk, 2 * kv_rows), jnp.bfloat16)] * 2
        + [shape((1, width), jnp.float32)],
        [*kv_parts, query_grad, *x_chunks, *w_chunks, cosine, sine, gain],
        [me],
        1,
    )


def input_backward(me, parts, layer_input, gain, middle_grad, count):
    rows, width = layer_input.shape
    chunk = width // count
    n = len(parts)

    def body(me_ref, x_ref, gain_ref, middle_ref, *refs):
        part = sum_parts([p[...] for p in refs[:n]])
        out_ref = refs[n]
        for r in range(count):
            out_ref[:, column(r, me_ref[0], chunk)] = part[:, r * chunk : (r + 1) * chunk]
        grad = out_ref[...]
        x = wide(x_ref[...])
        scale = lax.rsqrt(jnp.mean(x * x, axis=-1, keepdims=True) + epsilon)
        hat = x * scale
        weighted = grad * gain_ref[...]
        out_ref[...] = middle_ref[...] + scale * (
            weighted - hat * jnp.mean(weighted * hat, axis=-1, keepdims=True)
        )

    return call(
        body,
        [shape((rows, width), jnp.float32)],
        [layer_input, gain, middle_grad, *parts],
        [me],
        1,
    )[0]


def after(value, *others):
    return lax.optimization_barrier((value, *others))[0]


def layer_shards(
    layer_input,
    first_gain,
    query_weight,
    key_matrix,
    value_matrix,
    output_weight,
    second_gain,
    gate_weight,
    up_weight,
    down_weight,
    routes,
    combine,
    upstream,
):
    rows, width = layer_input.shape
    topk = routes.shape[1]
    most = max(2, 5 * rows * topk // (4 * EXPERTS))
    devices = lax.axis_size("dp")
    groups = lax.axis_size("mp")
    pieces_dev = gate_weight.shape[0]
    split = FF // gate_weight.shape[2]
    local_q = query_weight.shape[1] // HEAD_SIZE
    local_kv = key_matrix.shape[1] // HEAD_SIZE
    tokens = rows * groups
    span = SEQUENCE_TOKENS // tokens
    if span != devices or pieces_dev % 2 or groups % 2:
        return shards(
            layer_input, first_gain, query_weight, key_matrix, value_matrix, output_weight,
            second_gain, gate_weight, up_weight, down_weight, routes, combine, upstream,
        )
    dp_at, mp_at = lax.axis_index("dp"), lax.axis_index("mp")
    me = jnp.full((1,), dp_at, jnp.int32)
    offset = jnp.full((1,), dp_at % span, jnp.int32)
    gain_one, gain_two = first_gain.reshape(1, width), second_gain.reshape(1, width)

    chunk_at = jnp.arange(groups, dtype=jnp.int32) ^ mp_at
    inside = (chunk_at[:, None] * rows + jnp.arange(rows, dtype=jnp.int32)[None, :]).reshape(tokens)
    positions = (dp_at % span) * tokens + inside
    freqs = theta ** (-jnp.arange(HEAD_SIZE // 2, dtype=jnp.float32) * 2.0 / HEAD_SIZE)
    angles = freqs[:, None] * positions.astype(jnp.float32)[None, :]
    cosine, sine = jnp.cos(angles), jnp.sin(angles)

    numbers = jnp.arange(EXPERTS, dtype=jnp.int32)
    equal = routes.T[None, :, :] == numbers[:, None, None]
    match = jnp.sum(equal.astype(jnp.float32), axis=1)
    weight_table = jnp.sum(jnp.where(equal, combine.T[None, :, :], 0.0), axis=1)
    line = jnp.arange(rows, dtype=jnp.int32)
    earlier = (line[:, None] < line[None, :]).astype(jnp.bfloat16)
    rank = jnp.dot(match.astype(jnp.bfloat16), earlier, preferred_element_type=jnp.float32)
    terms = [low(jnp.where(match > 0, rank, -1.0))]
    rest = weight_table
    for _ in range(3):
        term = lax.reduce_precision(rest, 8, 7)
        terms.append(low(term))
        rest = rest - term
    table = jnp.stack(terms, axis=0)
    expert_at = (dp_at * pieces_dev + jnp.arange(pieces_dev, dtype=jnp.int32)) // split
    halves = pieces_dev // 2
    first_piece = (mp_at % 2) * halves
    order = (first_piece + jnp.arange(pieces_dev, dtype=jnp.int32)) % pieces_dev
    experts_order = jnp.take(expert_at, order)

    dp_order = jnp.arange(devices, dtype=jnp.int32) ^ dp_at

    selected = jnp.concatenate([dp_order, me, order])

    normed = first_norm_rows(layer_input, gain_one, me, devices)
    weight_cols = [w.shape[1] for w in (query_weight, key_matrix, value_matrix)]
    qkv_cols = sum(weight_cols)
    out_rows, out_cols = output_weight.shape
    payload = [query_weight, key_matrix, value_matrix, output_weight, table.reshape(out_rows, -1)]
    payloads = xor_gather(jnp.concatenate(payload, axis=1), "dp")
    qkv_chunks = (payloads, slice(0, qkv_cols))
    out_chunks = (payloads, slice(qkv_cols, qkv_cols + out_cols))
    tables = routing_tables(
        experts_order, payloads, slice(qkv_cols + out_cols, payloads[0].shape[1]), EXPERTS, most,
        pieces_dev,
    )
    x_chunks = xor_gather(normed, "mp")
    queries, kv_own = project(x_chunks, qkv_chunks, cosine, sine, local_q, local_kv)
    key_pos, query_pos = inside.reshape(tokens, 1), inside.reshape(1, tokens)
    kv_chunks, state, done = [kv_own] + [None] * (devices - 1), None, []
    forward_order = [(0,)] + [(r, r + 1) for r in range(1, devices - 1, 2)] + [(devices - 1,)]

    def attend(numbers, state):
        return attention_part(
            offset, state, queries, [kv_chunks[r] for r in numbers], numbers, key_pos, query_pos,
            local_q,
        )[0]

    for r in sorted(range(1, devices), key=lambda r: (bin(r).count("1"), -(r & -r))):
        near = r & -r
        source = kv_chunks[r ^ near]
        hops = bin(r).count("1") - 1
        if r > devices // 2 and hops > 0:
            while len(done) < hops:
                done.append(attend(forward_order[len(done)], state))
                state = done[-1]
            source = after(source, done[hops - 1])
        kv_chunks[r] = lax.ppermute(source, "dp", [(i, i ^ near) for i in range(devices)])
    for numbers in forward_order[len(done) :]:
        state = attend(numbers, state)
    gathered = lax.all_gather(after(upstream, kv_chunks[devices // 2]), "dp", axis=0, tiled=False)
    attended, lse, *branch_chunks = attention_end(state, out_chunks, local_q, kv_own.shape[0] // 2, groups)

    middle, second_norm = middle_rows(
        me, layer_input, xor_scatter(branch_chunks, "mp"), gain_two, devices
    )
    norm_chunks = xor_gather(second_norm, "dp")
    far_pairs = [[(i, i ^ g) for i in range(groups)] for g in range(2, groups, 2)]
    near_columns, later_columns = jnp.split(after(gathered, second_norm), 2, axis=2)
    columns_far = [lax.ppermute(near_columns, "mp", pairs) for pairs in far_pairs]
    expert_weights = (gate_weight, up_weight, down_weight)
    own = experts(
        selected, norm_chunks, [gathered], tables,
        *expert_weights, most, pieces_dev, True,
    )
    mixture, mixture_odd, back_chunks = own[2], own[3], own[4:]
    swap = [(i, i ^ 1) for i in range(groups)]
    fields = [own[0], lax.ppermute(own[1], "mp", swap)]
    back_parts = xor_scatter(back_chunks, "dp")
    middle_grad, branch_low, second_sum = middle_backward(
        me, back_parts, middle, gain_two, upstream, devices
    )

    branch_rows = xor_gather(branch_low, "mp")
    norm_here = after(stacked(norm_chunks), branch_rows[-1], *columns_far)
    later_columns = after(later_columns, branch_rows[-1], *columns_far)
    far_groups = [
        ([first, lax.ppermute(later_columns, "mp", pairs)],
         *[lax.ppermute(v, "mp", pairs) for v in (norm_here, tables)])
        for first, pairs in zip(columns_far, far_pairs)
    ]
    def halved(odd, even, bit):
        came = lax.ppermute(odd, "dp", [(i, i ^ bit) for i in range(devices)])
        return (wide(even) + wide(came)).astype(jnp.bfloat16)

    def halving(chunks):
        sums, bit = [halved(chunks[1], chunks[0], 1)], 2
        while bit < devices:
            sums.append(halved(sums[-1][1::2], sums[-1][0::2], bit))
            bit *= 2
        return sums

    mixture = halved(after(mixture_odd, branch_low), mixture, 1)
    started = attention_backward_start(
        queries, attended, [after(branch_rows[0], mixture), *branch_rows[1:]], out_chunks, local_q
    )
    odd = list(range(devices - 1, 0, -2))
    even = sorted(range(0, devices, 2), key=lambda r: (-bin(r).count("1"), -r))
    backward_order = [tuple(part[i : i + 2]) for part in (odd, even) for i in range(0, len(part), 2)]
    total, pending, waiting = None, [[] for _ in range(devices)], set(range(1, devices))
    computed, arrivals, bit = set(), [], 2
    for step, numbers in enumerate(backward_order):
        last = numbers is backward_order[-1]
        if step > 1:
            total = after(total, arrivals[step - 2])
            if bit < devices:
                mixture = halved(mixture[1::2], mixture[0::2], bit)
                total = after(total, mixture)
                bit *= 2
        total, *parts = attention_backward_part(
            offset, total, queries, [kv_chunks[r] for r in numbers], numbers, key_pos, query_pos,
            lse, started, local_q, (cosine, sine) if last else (),
        )
        for r, part in zip(numbers, parts):
            pending[r].insert(0, part)
            computed.add(r)
        for r in sorted(waiting, key=lambda r: (r % 2 == 0, -r)):
            near = r & -r
            feeders = [r | bit for bit in range(1, near) if bin(bit).count("1") == 1]
            if r in computed and not waiting.intersection(feeders):
                waiting.remove(r)
                came = lax.ppermute(
                    add_parts(pending[r]), "dp", [(i, i ^ near) for i in range(devices)]
                )
                pending[r ^ near].append(came)
                arrivals.append(came)
    query_plain, kv_parts = total, pending[0]
    while bit < devices:
        mixture = halved(mixture[1::2], mixture[0::2], bit)
        bit *= 2
    layer_output = (middle + wide(mixture[0])).astype(jnp.bfloat16)
    row_weights = row_grads([(x_chunks, query_plain), (branch_rows, attended)], devices)
    row_sums = halving(row_weights)
    places = jnp.stack([first_piece, jnp.int32(0)])
    fields[0] = after(fields[0], row_weights[0])
    totals = expert_weight_grads(places, halves, fields, [], pieces_dev, FF // split, False)
    kv_parts[0] = after(kv_parts[0], totals[0], row_sums[0])
    outs = input_parts(
        me, kv_parts, query_plain, x_chunks, qkv_chunks, cosine, sine, gain_one, local_kv, devices
    )
    in_chunks, kv_weights, first_sum = outs[:groups], outs[groups : groups + 2], outs[-1]
    kv_sums = halving(kv_weights)
    in_parts, hops = [in_chunks[0]], []
    pending = [[chunk] for chunk in in_chunks]
    for r in sorted(range(1, groups), key=lambda r: (-bin(r).count("1"), r & -r)):
        near = r & -r
        came = lax.ppermute(add_parts(pending[r]), "mp", [(i, i ^ near) for i in range(groups)])
        pending[r ^ near].append(came)
        hops.append(came)
    in_parts = pending[0]
    gains = jnp.concatenate([first_sum, second_sum], axis=0)

    def gain_hop(gains, axis, bit):
        count = lax.axis_size(axis)
        return gains + lax.ppermute(gains, axis, [(i, i ^ bit) for i in range(count)])

    steps = [(axis, 1 << i) for axis in ("mp", "dp") for i in range(8) if 1 << i < lax.axis_size(axis)]
    far_fields = []
    for rows_far, norm_far, tables_far in far_groups:
        kept, sent = experts(
            selected, [after(norm_far, first_sum)], rows_far, tables_far,
            *expert_weights, most, pieces_dev, False,
        )
        gains = gain_hop(gains, *steps.pop(0))
        far_fields += [kept, lax.ppermute(sent, "mp", swap)]
    received = []
    for i in range(halves):
        gains = gain_hop(gains, *steps.pop(0))
        places = jnp.stack([first_piece + i, jnp.int32(i)])
        hold = [hops[0], row_sums[1], kv_sums[0]] if i == 0 else [hops[-1], row_sums[-1], kv_sums[1]]
        far_fields[0] = after(far_fields[0], *hold, gains)
        *totals, sent = expert_weight_grads(
            places, 1, far_fields, totals, pieces_dev, FF // split, True
        )
        received.append(lax.ppermute(sent, "mp", swap))
    input_grad = input_backward(me, in_parts, layer_input, gain_one, middle_grad, devices)
    gains = gain_hop(after(gains, input_grad), *steps.pop(0))
    received[0] = after(received[0], kv_sums[-1])
    for i in range(halves):
        place = jnp.full((1,), halves - first_piece + i, jnp.int32)
        totals = fill_pieces(place, totals, received[i])
        if steps:
            gains = gain_hop(after(gains, totals[0]), *steps.pop(0))
    for step in steps:
        gains = gain_hop(gains, *step)
    gate_grad, up_grad, down_grad = totals
    row_weight_grad, kv_grad = wide(row_sums[-1][0]), wide(kv_sums[-1][0])
    query_cols, kv_cols = local_q * HEAD_SIZE, local_kv * HEAD_SIZE
    first_gain_grad, second_gain_grad = gains[0], gains[1]
    return (
        layer_output,
        input_grad,
        first_gain_grad,
        second_gain_grad,
        row_weight_grad[:, :query_cols],
        kv_grad[:, :kv_cols],
        kv_grad[:, kv_cols:],
        row_weight_grad[:, query_cols:],
        gate_grad,
        up_grad,
        down_grad,
    )


def solution(mesh):
    in_specs = (
        P(("dp", "mp"), None),
        P(),
        P("dp", "mp"),
        P("dp", "mp"),
        P("dp", "mp"),
        P("dp", "mp"),
        P(),
        P("dp", None, None),
        P("dp", None, None),
        P("dp", None, None),
        P(("dp", "mp"), None),
        P(("dp", "mp"), None),
        P(("dp", "mp"), None),
    )
    out_specs = (
        P(("dp", "mp"), None),
        P(("dp", "mp"), None),
        P(),
        P(),
        P("dp", "mp"),
        P("dp", "mp"),
        P("dp", "mp"),
        P("dp", "mp"),
        P("dp", None, None),
        P("dp", None, None),
        P("dp", None, None),
    )
    return jax.shard_map(
        layer_shards, mesh=mesh, in_specs=in_specs, out_specs=out_specs, check_vma=False)
```
